256 devices in a mesh: adapter: 8 (over z), tensor: 32 (over y, x, core).
Axes of the slice: x: 4, y: 4, z: 8, core: 2. Of those that a mesh axis runs over, the one named last changes fastest.
Arguments:
- hidden_activations: bfloat16 [2048, 16384], P('adapter', 'tensor'), may hold values from -6 to 6
- cotangent: bfloat16 [2048, 8192], P('adapter'), may hold values from -1.5 to 1.5
- shadow_assignment: int32 [2048], P('adapter'), may hold values from 0 to 63, as said below
- frozen_down_weight: bfloat16 [16384, 8192], P('tensor'), may hold values from -0.046875 to 0.046875
- adapter_down_factors: bfloat16 [64, 16, 16384], P('adapter', None, 'tensor'), may hold values from -0.046875 to 0.046875
- adapter_up_factors: bfloat16 [64, 16, 8192], P('adapter', None, 'tensor'), may hold values from -1.5 to 1.5
Outputs:
- mixed: bfloat16 [2048, 8192], P('adapter')
- hidden_input_gradient: bfloat16 [2048, 16384], P('adapter', 'tensor')
- down_factor_gradient: float32 [64, 16, 16384], P('adapter', None, 'tensor')
- up_factor_gradient: float32 [64, 16, 8192], P('adapter', None, 'tensor')
The draws below stay inside these ranges and needn't reach their ends.
Inputs may be any that keep to these rules, and one draw needn't show every extreme that they name: `shadow_assignment`: the shadows fall into groups of 8 consecutive numbers. Among the 256 tokens of each aligned block (the tokens of one device) at most 128 belong to one group; one group, the same in every block, has exactly 128 tokens in every block.
All inputs are finite; a program needn't handle non-finite values.
Results may differ from the reference program's by a relative error of at most 0.0038.
Values may be sent and summed in bfloat16 or wider, within the bound.
A program may use at most 128 MiB of HBM per device.

```python
import jax
import jax.numpy as jnp

MODEL_WIDTH = 8192
HIDDEN_UNITS = 16384
ADAPTER_RANK = 16
SHADOW_DEV = 8
TOK_DEV = 256
SHADOW_MODELS = 64
TOKENS = 2048
CAP = 128


def shuffle_block(block_key):
    return jax.random.permutation(block_key, TOK_DEV)


def draw_shadow_assignment(key, part):
    key = jax.random.fold_in(key, 11)
    group_total = SHADOW_MODELS // SHADOW_DEV
    block_total = TOKENS // TOK_DEV
    key_list = jax.random.split(key, 4)
    heavy_group = jax.random.randint(key_list[0], (), 0, group_total)
    others = (heavy_group + 1 + jax.random.randint(key_list[1], (block_total, TOK_DEV - CAP), 0, group_total - 1)) % group_total
    groups = jnp.concatenate([jnp.full((block_total, CAP), heavy_group, jnp.int32), others.astype(jnp.int32)], axis=1)
    shuffles = jax.vmap(shuffle_block)(jax.random.split(key_list[2], block_total))
    groups = jnp.take_along_axis(groups, shuffles, axis=1)
    members = jax.random.randint(key_list[3], (block_total, TOK_DEV), 0, SHADOW_DEV)
    return (groups * SHADOW_DEV + members).reshape(TOKENS).astype(jnp.int32)


def block_levels(rng, dims, cuts, least, largest):
    loudness, own = 1.0, jax.random.fold_in(rng, 6)
    for position, shards_of in cuts:
        heights = jnp.exp(jax.random.uniform(jax.random.fold_in(own, position), (shards_of,), jnp.float32, least / len(cuts), largest / len(cuts)))
        loudness = loudness * jnp.repeat(heights, dims[position] // shards_of).reshape([-1 if axis == position else 1 for axis in range(len(dims))])
    return loudness


def normal_values(own_key, extent, width, reach, cuts=(), held_as=jnp.bfloat16):
    values = width * jax.random.normal(own_key, extent, jnp.float32)
    if cuts:
        values = values * block_levels(own_key, extent, cuts, -0.22, 0.18)
    return jnp.clip(values, -reach, reach).astype(held_as)


def setup_inputs(seed: int = 0) -> dict:
    splits = jax.random.split(jax.random.key(seed), 7)
    return {
        "hidden_activations": normal_values(splits[0], (TOKENS, HIDDEN_UNITS), 1.0, 6.0, ((0, 8), (1, 32))),
        "cotangent": normal_values(splits[1], (TOKENS, MODEL_WIDTH), 0.25, 1.5, ((0, 8),)),
        "shadow_assignment": draw_shadow_assignment(jax.random.fold_in(splits[6], 71), 0),
        "frozen_down_weight": normal_values(splits[3], (HIDDEN_UNITS, MODEL_WIDTH), HIDDEN_UNITS ** -0.5, 0.046875, ((0, 32),)),
        "adapter_down_factors": normal_values(splits[4], (SHADOW_MODELS, ADAPTER_RANK, HIDDEN_UNITS), HIDDEN_UNITS ** -0.5, 0.046875, ((0, 8), (2, 32))),
        "adapter_up_factors": normal_values(splits[5], (SHADOW_MODELS, ADAPTER_RANK, MODEL_WIDTH), ADAPTER_RANK ** -0.5, 1.5, ((0, 8), (2, 32))),
    }


def reference(hidden_activations, cotangent, shadow_assignment, frozen_down_weight, adapter_down_factors, adapter_up_factors):
    selector = (shadow_assignment[:, None] == jnp.arange(SHADOW_MODELS, dtype=jnp.int32)[None, :])
    select_f = selector.astype(jnp.float32)
    select_b = selector.astype(jnp.bfloat16)
    down_factor_flat = adapter_down_factors.reshape(SHADOW_MODELS * ADAPTER_RANK, HIDDEN_UNITS)
    up_factor_flat = adapter_up_factors.reshape(SHADOW_MODELS * ADAPTER_RANK, MODEL_WIDTH)
    low_all = jnp.dot(hidden_activations, down_factor_flat.T, preferred_element_type=jnp.float32)
    low_all = low_all.reshape(TOKENS, SHADOW_MODELS, ADAPTER_RANK)
    low = jnp.sum(low_all * select_f[:, :, None], axis=1).astype(jnp.bfloat16)
    back_all = jnp.dot(cotangent, up_factor_flat.T, preferred_element_type=jnp.float32)
    back_all = back_all.reshape(TOKENS, SHADOW_MODELS, ADAPTER_RANK)
    back_low = jnp.sum(back_all * select_f[:, :, None], axis=1).astype(jnp.bfloat16)
    reduced_sparse_rows = (select_b[:, :, None] * low[:, None, :]).reshape(TOKENS, SHADOW_MODELS * ADAPTER_RANK)
    backward_sparse_rows = (select_b[:, :, None] * back_low[:, None, :]).reshape(TOKENS, SHADOW_MODELS * ADAPTER_RANK)
    mixed = jnp.dot(hidden_activations, frozen_down_weight, preferred_element_type=jnp.float32)
    mixed = mixed + jnp.dot(reduced_sparse_rows, up_factor_flat, preferred_element_type=jnp.float32)
    hidden_input_gradient = jnp.dot(cotangent, frozen_down_weight.T, preferred_element_type=jnp.float32)
    hidden_input_gradient = hidden_input_gradient + jnp.dot(backward_sparse_rows, down_factor_flat, preferred_element_type=jnp.float32)
    down_factor_gradient = jnp.dot(backward_sparse_rows.T, hidden_activations, preferred_element_type=jnp.float32)
    up_factor_gradient = jnp.dot(reduced_sparse_rows.T, cotangent, preferred_element_type=jnp.float32)
    return (mixed.astype(jnp.bfloat16), hidden_input_gradient.astype(jnp.bfloat16),
            down_factor_gradient.reshape(SHADOW_MODELS, ADAPTER_RANK, HIDDEN_UNITS), up_factor_gradient.reshape(SHADOW_MODELS, ADAPTER_RANK, MODEL_WIDTH))
```

```python
import jax
import jax.numpy as jnp
from jax import lax
from jax.experimental import pallas as pl
from jax.experimental.pallas import tpu as pltpu
from jax.sharding import PartitionSpec as P

BF = jnp.bfloat16
F32 = jnp.float32
MESH = pl.DeviceIdType.MESH
NSEM = 160
OFFS = (2, 1, 3, 0)


def nt(left, right):
    return lax.dot_general(left, right, (((1,), (1,)), ((), ())), preferred_element_type=F32)


def tn(left, right):
    return lax.dot_general(left, right, (((0,), (0,)), ((), ())), preferred_element_type=F32)


def nn(left, right):
    return lax.dot_general(left, right, (((1,), (0,)), ((), ())), preferred_element_type=F32)


def kernel(
    x_hbm, g_hbm, ids_ref, w_hbm, ad_hbm, au_hbm,
    mixed, hg_out, dg_out, ug_out,
    xv, gs, gv, wv, adv, auv,
    own, sib_tx, sib_rx, rs_tx, rs_rx, r_buf, p2_tx, p2_rx, fb,
    hg_acc, hg_bf, lr_acc, lr_tx, lr_rx, sel, zr_own, zr_tx, zr_rx, dg_buf, ug_buf,
    lsem, wsem, gsem, ssem, rsem,
):
    z = lax.axis_index("adapter")
    t = lax.axis_index("tensor")
    c = lax.rem(t, 2)
    x = lax.rem(lax.div(t, 2), 4)
    y = lax.div(t, 8)
    d = 1 - c
    p = x * d + y * c
    q = y * d + x * c

    def tid(pp, qq, cc):
        return lax.rem(pp, 4) * (2 + 6 * cc) + lax.rem(qq, 4) * (8 - 6 * cc) + cc

    def cols(block):
        return pl.ds(pl.multiple_of(block * 256, 256), 256)

    sib = (z, t + 1 - 2 * c)

    def at_p(k):
        return (z, tid(p + k, q, c))

    def at_q(k):
        return (z, tid(p, q + k, c))

    def at_x(k):
        return (z, (y * 4 + lax.rem(x + k, 4)) * 2 + c)

    def at_y(k):
        return (z, (lax.rem(y + k, 4) * 4 + x) * 2 + c)

    zp = (lax.rem(z + 1, 8), t)
    zm = (lax.rem(z + 7, 8), t)

    def slot(k):
        return lax.rem(z + k + 8, 8)

    count = [0]
    sent = []

    def send(src, dst, device):
        i = count[0]
        count[0] += 1
        cp = pltpu.make_async_remote_copy(
            src_ref=src, dst_ref=dst, send_sem=ssem.at[i], recv_sem=rsem.at[i],
            device_id=device, device_id_type=MESH,
        )
        cp.start()
        sent.append(cp)
        return cp

    def load(src, dst, sem):
        cp = pltpu.make_async_copy(src, dst, sem)
        cp.start()
        return cp

    ld_x = load(x_hbm, xv, lsem.at[0])

    def group_block(g, j):
        k, mine = g // 2, g % 2
        if mine:
            return tid(p + OFFS[k], j, c)
        return tid(q + OFFS[k], j, d)

    ld_w = [
        [load(w_hbm.at[:, cols(group_block(g, j))], wv.at[g, :, pl.ds(j * 256, 256)], wsem.at[g * 4 + j])
         for j in range(4)] for g in range(8)
    ]
    ld_ad = load(ad_hbm, adv.at[z], lsem.at[1])
    ld_au = load(au_hbm, auv.at[z], lsem.at[2])
    ld_gs = load(g_hbm.at[:, cols(t)], gs, lsem.at[3])
    ld_g = [
        [load(g_hbm.at[:, cols(group_block(g, j))], gv.at[g, :, pl.ds(j * 256, 256)], gsem.at[g * 4 + j])
         for j in range(4)] for g in range(8)
    ]

    bar = pltpu.get_barrier_semaphore()
    for dev in [sib, zp, zm] + [at_x(k) for k in (1, 2, 3)] + [at_y(k) for k in (1, 2, 3)]:
        pl.semaphore_signal(bar, inc=1, device_id=dev, device_id_type=MESH)

    def matmul_round(k):
        for mine in (0, 1):
            g = 2 * k + mine
            for cp in ld_w[g]:
                cp.wait()

            def body(j, carry):
                at = pl.ds(pl.multiple_of(j * 256, 256), 256)
                res = nn(xv[...], wv[g, :, at])
                if mine:
                    own[k, :, at] = res
                else:
                    sib_tx[k, :, at] = res.astype(BF)
                return carry

            lax.fori_loop(0, 4, body, 0)

    ld_x.wait()
    matmul_round(0)
    pl.semaphore_wait(bar, 9)

    def ad0(s, rows=slice(None)):
        return adv.at[s, rows, pl.ds(0, 256)]

    def ad1(s, rows=slice(None)):
        return adv.at[s, rows, pl.ds(256, 256)]

    def au0(s, rows=slice(None)):
        return auv.at[s, rows, :]

    TOP, LOW = pl.ds(0, 64), pl.ds(64, 64)

    def ag_first(view, hbm):
        return send(hbm, view(z), zp), send(hbm, view(z), zm)

    def ag_next(view, prev, k):
        prev[0].wait_recv()
        prev[1].wait_recv()
        if k == 5:
            return None
        if k == 4:
            return (
                send(view(slot(-3), TOP), view(slot(-3), TOP), zp),
                send(view(slot(3), LOW), view(slot(3), LOW), zm),
            )
        a, b = slot(1 - k), slot(k - 1)
        return send(view(a), view(a), zp), send(view(b), view(b), zm)

    h0 = ag_first(ad0, ad_hbm.at[:, pl.ds(0, 256)])
    h1 = ag_first(ad1, ad_hbm.at[:, pl.ds(256, 256)])
    hu = ag_first(au0, au_hbm)

    def sib_send(k):
        return send(sib_tx.at[k], sib_rx.at[k], sib)

    def sib_add(k):
        own[k] = own[k] + sib_rx[k].astype(F32)

    s0 = sib_send(0)
    matmul_round(1)
    s1 = sib_send(1)
    s0.wait_recv()
    rs_tx[0] = (own[0, 0:128] + sib_rx[0, 0:128].astype(F32)).astype(BF)
    a_p = send(rs_tx.at[0], rs_rx.at[0], at_p(1))
    rs_tx[1] = (own[0, 128:256] + sib_rx[0, 128:256].astype(F32)).astype(BF)
    a_m = send(rs_tx.at[1], rs_rx.at[1], at_p(3))
    matmul_round(2)
    s2 = sib_send(2)
    h0 = ag_next(ad0, h0, 2)
    s1.wait_recv()
    sib_add(1)
    rs_tx[2] = own[1, 128:256].astype(BF)
    b_p = send(rs_tx.at[2], rs_rx.at[2], at_p(1))
    h1 = ag_next(ad1, h1, 2)
    s2.wait_recv()
    sib_add(2)
    rs_tx[3] = own[2, 0:128].astype(BF)
    b_m = send(rs_tx.at[3], rs_rx.at[3], at_p(3))
    matmul_round(3)
    s3 = sib_send(3)
    hu = ag_next(au0, hu, 2)

    def mask(s):
        want = lax.broadcasted_iota(jnp.int32, (8, 1, 256), 0) + s * 8
        return want == ids_ref[...].reshape(1, 1, 256)

    def project(which, s):
        if which == 0:
            full = nt(adv[s], xv[...])
        else:
            full = nt(auv[s], gs[...])
        lr_acc[which] += jnp.sum(jnp.where(mask(s), full.reshape(8, 16, 256), 0.0), axis=0)

    lr_acc[...] = jnp.zeros_like(lr_acc)
    ld_ad.wait()
    project(0, z)
    s3.wait_recv()
    sib_add(3)
    a_p.wait_recv()
    rs_tx[4] = (own[1, 0:128] + rs_rx[0].astype(F32)).astype(BF)
    c_p = send(rs_tx.at[4], rs_rx.at[4], at_p(1))
    a_m.wait_recv()
    rs_tx[5] = (own[2, 128:256] + rs_rx[1].astype(F32)).astype(BF)
    c_m = send(rs_tx.at[5], rs_rx.at[5], at_p(3))
    h0 = ag_next(ad0, h0, 3)
    project(0, slot(1))
    project(0, slot(7))

    def backward(lo, hi, first):
        for g in range(lo, hi):
            for cp in ld_g[g]:
                cp.wait()
        if first:
            hg_acc[...] = jnp.zeros_like(hg_acc)

        def body(g, carry):
            hg_acc[...] += nt(gv[g], wv[g])
            return carry

        lax.fori_loop(lo, hi, body, 0)

    backward(0, 2, True)
    h1 = ag_next(ad1, h1, 3)
    project(0, slot(2))
    project(0, slot(6))
    hu = ag_next(au0, hu, 3)
    backward(2, 4, False)
    h0 = ag_next(ad0, h0, 4)
    b_m.wait_recv()
    b_p.wait_recv()
    c_p.wait_recv()
    r_buf[0:128] = own[3, 0:128] + rs_rx[3].astype(F32) + rs_rx[4].astype(F32)
    c_m.wait_recv()
    r_buf[128:256] = own[3, 128:256] + rs_rx[2].astype(F32) + rs_rx[5].astype(F32)

    p2 = []
    for k in (1, 3, 2):
        p2_tx[k - 1] = r_buf[:, cols(lax.rem(q + k, 4))].astype(BF)
        p2.append(send(p2_tx.at[k - 1], p2_rx.at[k - 1], at_q(k)))
    h1 = ag_next(ad1, h1, 4)
    project(0, slot(3))
    project(0, slot(5))
    hu = ag_next(au0, hu, 4)
    h0 = ag_next(ad0, h0, 5)
    h1 = ag_next(ad1, h1, 5)
    project(0, slot(4))

    def psum_start(which, stage):
        lr_tx[which, stage] = lr_acc[which]
        src = lr_tx.at[which, stage]
        if stage == 0:
            return [send(src, lr_rx.at[which, 0], sib)]
        at = at_x if stage == 1 else at_y
        return [send(src, lr_rx.at[which, 3 * stage - 3 + k], at(k)) for k in (1, 2, 3)]

    def psum_end(which, stage, cps):
        for cp in cps:
            cp.wait_recv()
        if stage == 0:
            lr_acc[which] += lr_rx[which, 0]
        else:
            b = 3 * stage - 3
            lr_acc[which] += lr_rx[which, b + 1] + lr_rx[which, b + 2] + lr_rx[which, b + 3]

    lp = psum_start(0, 0)
    ld_au.wait()
    ld_gs.wait()
    project(1, z)
    project(1, slot(1))
    project(1, slot(7))
    psum_end(0, 0, lp)
    lp = psum_start(0, 1)
    project(1, slot(2))
    project(1, slot(6))
    project(1, slot(3))
    project(1, slot(5))
    backward(4, 6, False)
    for cp in p2:
        cp.wait_recv()
    hu = ag_next(au0, hu, 5)
    project(1, slot(4))
    bp = psum_start(1, 0)
    psum_end(0, 1, lp)
    lp = psum_start(0, 2)
    psum_end(1, 0, bp)
    bp = psum_start(1, 1)
    backward(6, 8, False)
    f_pre = (
        r_buf[:, cols(q)] + p2_rx[0].astype(F32) + p2_rx[1].astype(F32) + p2_rx[2].astype(F32)
    )
    r_buf[:, 0:256] = f_pre
    psum_end(0, 2, lp)

    def select(which):
        low = lr_acc[which].astype(BF).astype(F32)[None]
        for s in range(8):
            sel[which, pl.ds(s * 128, 128)] = (
                jnp.where(mask(s), low, 0.0).reshape(128, 256).astype(BF)
            )

    select(0)
    adapted = tn(sel[0], auv[...].reshape(1024, 256))
    fb[...] = (r_buf[:, 0:256] + adapted).astype(BF)

    def gather(block, device, rows=slice(None)):
        ref = mixed.at[rows, cols(block)]
        return send(ref, ref, device)

    mine = tid(p, q, c)
    own_out = mixed.at[:, cols(mine)]
    ag_p = {}
    ag_m = {}
    ag_p[0] = send(fb, own_out, at_p(1))
    ag_m[0] = send(fb, own_out, at_p(3))
    ag_q = {k: send(fb, own_out, at_q(k)) for k in (1, 3, 2)}
    sibs = [send(fb, own_out, sib)]
    ld_own = load(fb, own_out, lsem.at[4])

    def grad_part(chain, s):
        rows = pl.ds(pl.multiple_of(s * 128, 128), 128)
        if chain == 0:
            return nn(sel[0, rows], gs[...])
        return nn(sel[1, rows], xv[:, (chain - 1) * 256:chain * 256])

    def rs_start(chain):
        zr_tx[chain, 0] = grad_part(chain, slot(4)).astype(BF)
        hp = send(zr_tx.at[chain, 0, TOP], zr_rx.at[chain, 0, TOP], zp)
        hm = send(zr_tx.at[chain, 0, LOW], zr_rx.at[chain, 0, LOW], zm)
        for k in (3, 2, 1):
            zr_own[chain, 3 - k] = grad_part(chain, slot(k))
            zr_own[chain, 6 - k] = grad_part(chain, slot(-k))
        zr_own[chain, 6] = grad_part(chain, z)
        return hp, hm

    def rs_next(chain, step, prev):
        prev[0].wait_recv()
        if step == 1:
            zr_tx[chain, 1, TOP] = (zr_own[chain, 0, TOP] + zr_rx[chain, 0, TOP].astype(F32)).astype(BF)
            zr_tx[chain, 1, LOW] = zr_own[chain, 0, LOW].astype(BF)
        else:
            zr_tx[chain, step] = (zr_own[chain, step - 1] + zr_rx[chain, step - 1].astype(F32)).astype(BF)
        hp = send(zr_tx.at[chain, step], zr_rx.at[chain, step], zp)
        prev[1].wait_recv()
        if step == 1:
            zr_tx[chain, 4, TOP] = zr_own[chain, 3, TOP].astype(BF)
            zr_tx[chain, 4, LOW] = (zr_own[chain, 3, LOW] + zr_rx[chain, 0, LOW].astype(F32)).astype(BF)
        else:
            zr_tx[chain, 3 + step] = (
                zr_own[chain, 2 + step] + zr_rx[chain, 2 + step].astype(F32)
            ).astype(BF)
        hm = send(zr_tx.at[chain, 3 + step], zr_rx.at[chain, 3 + step], zm)
        return hp, hm

    def rs_end(chain, prev):
        prev[0].wait_recv()
        prev[1].wait_recv()
        return zr_own[chain, 6] + zr_rx[chain, 3].astype(F32) + zr_rx[chain, 6].astype(F32)

    cu = rs_start(0)
    psum_end(1, 1, bp)
    bp = psum_start(1, 2)

    def spread(k):
        ag_p[k].wait_recv()
        bm = tid(p + 3, q + k, c)
        f1 = gather(bm, at_p(1), pl.ds(0, 128))
        sibs.append(gather(bm, sib))
        ag_m[k].wait_recv()
        bq = tid(p + 1, q + k, c)
        f2 = gather(bq, at_p(3), pl.ds(128, 128))
        sibs.append(gather(bq, sib))
        return f1, f2

    halves = {}
    halves[0] = spread(0)
    for k in (1, 3, 2):
        ag_q[k].wait_recv()
        blk = tid(p, q + 4 - k, c)
        ag_p[4 - k] = gather(blk, at_p(1))
        ag_m[4 - k] = gather(blk, at_p(3))
        sibs.append(gather(blk, sib))
        if k == 3:
            cu = rs_next(0, 1, cu)
    psum_end(1, 2, bp)
    select(1)
    c0 = rs_start(1)
    c1 = rs_start(2)
    hg_bf[...] = (hg_acc[...] + tn(sel[1], adv[...].reshape(1024, 512))).astype(BF)
    st_hg = load(hg_bf, hg_out, lsem.at[5])
    cu = rs_next(0, 2, cu)
    halves[3] = spread(3)
    c0 = rs_next(1, 1, c0)
    c1 = rs_next(2, 1, c1)
    halves[1] = spread(1)
    cu = rs_next(0, 3, cu)
    c0 = rs_next(1, 2, c0)
    c1 = rs_next(2, 2, c1)
    halves[2] = spread(2)
    for k in (0, 3, 1, 2):
        f1, f2 = halves[k]
        blk = tid(p + 2, q + k, c)
        f1.wait_recv()
        f2.wait_recv()
        sibs.append(gather(blk, sib))
    ug_buf[...] = rs_end(0, cu)
    st_ug = load(ug_buf, ug_out, lsem.at[6])
    c0 = rs_next(1, 3, c0)
    c1 = rs_next(2, 3, c1)
    for cp in sibs:
        cp.wait_recv()
    dg_buf[:, 0:256] = rs_end(1, c0)
    dg_buf[:, 256:512] = rs_end(2, c1)
    st_dg = load(dg_buf, dg_out, lsem.at[7])
    for cp in sent:
        cp.wait_send()
    for cp in (ld_own, st_hg, st_ug, st_dg):
        cp.wait()


def on_device(x, g, ids, w, ad, au):
    any_spec = pl.BlockSpec(memory_space=pl.ANY)
    vmem = pl.BlockSpec(memory_space=pltpu.VMEM)
    mixed, hg, dg, ug = pl.pallas_call(
        kernel,
        out_shape=(
            jax.ShapeDtypeStruct((256, 8192), BF),
            jax.ShapeDtypeStruct((256, 512), BF),
            jax.ShapeDtypeStruct((128, 512), F32),
            jax.ShapeDtypeStruct((128, 256), F32),
        ),
        in_specs=[any_spec, any_spec, vmem, any_spec, any_spec, any_spec],
        out_specs=(any_spec,) * 4,
        scratch_shapes=[
            pltpu.VMEM((256, 512), BF),
            pltpu.VMEM((256, 256), BF),
            pltpu.VMEM((8, 256, 1024), BF),
            pltpu.VMEM((8, 512, 1024), BF),
            pltpu.VMEM((8, 128, 512), BF),
            pltpu.VMEM((8, 128, 256), BF),
            pltpu.VMEM((4, 256, 1024), F32),
            pltpu.VMEM((4, 256, 1024), BF),
            pltpu.VMEM((4, 256, 1024), BF),
            pltpu.VMEM((6, 128, 1024), BF),
            pltpu.VMEM((6, 128, 1024), BF),
            pltpu.VMEM((256, 1024), F32),
            pltpu.VMEM((3, 256, 256), BF),
            pltpu.VMEM((3, 256, 256), BF),
            pltpu.VMEM((256, 256), BF),
            pltpu.VMEM((256, 512), F32),
            pltpu.VMEM((256, 512), BF),
            pltpu.VMEM((2, 16, 256), F32),
            pltpu.VMEM((2, 3, 16, 256), F32),
            pltpu.VMEM((2, 7, 16, 256), F32),
            pltpu.VMEM((2, 1024, 256), BF),
            pltpu.VMEM((3, 7, 128, 256), F32),
            pltpu.VMEM((3, 7, 128, 256), BF),
            pltpu.VMEM((3, 7, 128, 256), BF),
            pltpu.VMEM((128, 512), F32),
            pltpu.VMEM((128, 256), F32),
            pltpu.SemaphoreType.DMA((8,)),
            pltpu.SemaphoreType.DMA((32,)),
            pltpu.SemaphoreType.DMA((32,)),
            pltpu.SemaphoreType.DMA((NSEM,)),
            pltpu.SemaphoreType.DMA((NSEM,)),
        ],
        compiler_params=pltpu.CompilerParams(
            collective_id=0, has_side_effects=True, vmem_limit_bytes=56 * 2**20
        ),
    )(x, g, ids.reshape(1, 256), w, ad.reshape(128, 512), au.reshape(128, 256))
    return mixed, hg, dg.reshape(8, 16, 512), ug.reshape(8, 16, 256)


def solution(mesh):
    return jax.shard_map(
        on_device,
        mesh=mesh,
        in_specs=(
            P("adapter", "tensor"),
            P("adapter", None),
            P("adapter"),
            P("tensor", None),
            P("adapter", None, "tensor"),
            P("adapter", None, "tensor"),
        ),
        out_specs=(
            P("adapter", None),
            P("adapter", "tensor"),
            P("adapter", None, "tensor"),
            P("adapter", None, "tensor"),
        ),
        check_vma=False,
    )
```

```python
import jax
import jax.numpy as jnp
from jax import lax
from jax.experimental import pallas as pl
from jax.experimental.pallas import tpu as pltpu
from jax.sharding import PartitionSpec as P

BF = jnp.bfloat16
F32 = jnp.float32
MESH = pl.DeviceIdType.MESH
NSEM = 160
OFFS = (2, 1, 3, 0)


def nt(left, right):
    return lax.dot_general(left, right, (((1,), (1,)), ((), ())), preferred_element_type=F32)


def tn(left, right):
    return lax.dot_general(left, right, (((0,), (0,)), ((), ())), preferred_element_type=F32)


def nn(left, right):
    return lax.dot_general(left, right, (((1,), (0,)), ((), ())), preferred_element_type=F32)


def kernel(
    x_hbm, g_hbm, ids_ref, w_hbm, ad_hbm, au_hbm,
    mixed, hg_out, dg_out, ug_out,
    xv, gs, gv, wv, adv, auv,
    own, sib_tx, sib_rx, rs_tx, rs_rx, r_buf, p2_tx, p2_rx, fb,
    hg_acc, hg_bf, lr_acc, lr_tx, lr_rx, sel, zr_own, zr_tx, zr_rx, dg_buf, ug_buf,
    lsem, wsem, gsem, ssem, rsem,
):
    z = lax.axis_index("adapter")
    t = lax.axis_index("tensor")
    c = lax.rem(t, 2)
    x = lax.rem(lax.div(t, 2), 4)
    y = lax.div(t, 8)
    d = 1 - c
    p = x * d + y * c
    q = y * d + x * c

    def tid(pp, qq, cc):
        return lax.rem(pp, 4) * (2 + 6 * cc) + lax.rem(qq, 4) * (8 - 6 * cc) + cc

    def cols(block):
        return pl.ds(pl.multiple_of(block * 256, 256), 256)

    sib = (z, t + 1 - 2 * c)

    def at_p(k):
        return (z, tid(p + k, q, c))

    def at_q(k):
        return (z, tid(p, q + k, c))

    def at_x(k):
        return (z, (y * 4 + lax.rem(x + k, 4)) * 2 + c)

    def at_y(k):
        return (z, (lax.rem(y + k, 4) * 4 + x) * 2 + c)

    zp = (lax.rem(z + 1, 8), t)
    zm = (lax.rem(z + 7, 8), t)

    def slot(k):
        return lax.rem(z + k + 8, 8)

    count = [0]
    sent = []

    def send(src, dst, device):
        i = count[0]
        count[0] += 1
        cp = pltpu.make_async_remote_copy(
            src_ref=src, dst_ref=dst, send_sem=ssem.at[i], recv_sem=rsem.at[i],
            device_id=device, device_id_type=MESH,
        )
        cp.start()
        sent.append(cp)
        return cp

    def load(src, dst, sem):
        cp = pltpu.make_async_copy(src, dst, sem)
        cp.start()
        return cp

    ld_x = load(x_hbm, xv, lsem.at[0])

    def group_block(g, j):
        k, mine = g // 2, g % 2
        if mine:
            return tid(p + OFFS[k], j, c)
        return tid(q + OFFS[k], j, d)

    def load_w(g):
        return [
            load(w_hbm.at[:, cols(group_block(g, j))], wv.at[g, :, pl.ds(j * 256, 256)], wsem.at[g * 4 + j])
            for j in range(4)
        ]

    def load_g(g):
        return [
            load(g_hbm.at[:, cols(group_block(g, j))], gv.at[g, :, pl.ds(j * 256, 256)], gsem.at[g * 4 + j])
            for j in range(4)
        ]

    ld_w = [load_w(0), load_w(1)]

    bar = pltpu.get_barrier_semaphore()
    for dev in [sib, zp, zm] + [at_x(k) for k in (1, 2, 3)] + [at_y(k) for k in (1, 2, 3)]:
        pl.semaphore_signal(bar, inc=1, device_id=dev, device_id_type=MESH)

    def matmul_half(k, mine):
        g = 2 * k + mine
        for cp in ld_w[g]:
            cp.wait()

        for j in range(2):
            at = pl.ds(j * 512, 512)
            res = nn(xv[...], wv[g, :, at])
            if mine:
                own[k, :, at] = res
            else:
                sib_tx[k, :, at] = res.astype(BF)

    pl.semaphore_wait(bar, 9)

    def ad0(s, rows=slice(None)):
        return adv.at[s, rows, pl.ds(0, 256)]

    def ad1(s, rows=slice(None)):
        return adv.at[s, rows, pl.ds(256, 256)]

    def au0(s, rows=slice(None)):
        return auv.at[s, rows, :]

    TOP, LOW = pl.ds(0, 64), pl.ds(64, 64)

    def ag_first(view, hbm):
        return send(hbm, view(z), zp), send(hbm, view(z), zm)

    def ag_next(view, prev, k):
        prev[0].wait_recv()
        prev[1].wait_recv()
        if k == 5:
            return None
        if k == 4:
            return (
                send(view(slot(-3), TOP), view(slot(-3), TOP), zp),
                send(view(slot(3), LOW), view(slot(3), LOW), zm),
            )
        a, b = slot(1 - k), slot(k - 1)
        return send(view(a), view(a), zp), send(view(b), view(b), zm)

    def sib_part(k):
        matmul_half(k, 0)
        return send(sib_tx.at[k], sib_rx.at[k], sib)

    def mask(s):
        want = lax.broadcasted_iota(jnp.int32, (8, 1, 256), 0) + s * 8
        return want == ids_ref[...].reshape(1, 1, 256)

    def project(which, s):
        if which == 0:
            full = nt(adv[s], xv[...])
        else:
            full = nt(auv[s], gs[...])
        lr_acc[which] += jnp.sum(jnp.where(mask(s), full.reshape(8, 16, 256), 0.0), axis=0)

    def backward(lo, hi, first):
        for g in range(lo, hi):
            for cp in ld_g[g]:
                cp.wait()
        if first:
            hg_acc[...] = jnp.zeros_like(hg_acc)

        def body(g, carry):
            hg_acc[...] += nt(gv[g], wv[g])
            return carry

        lax.fori_loop(lo, hi, body, 0)

    def psum_start(stage):
        lr_tx[stage] = lr_acc[...]
        src = lr_tx.at[stage]
        if stage == 0:
            return [send(src, lr_rx.at[0], sib)]
        at = at_x if stage == 1 else at_y
        return [send(src, lr_rx.at[3 * stage - 3 + k], at(k)) for k in (1, 3, 2)]

    def psum_end(stage, cps):
        for cp in cps:
            cp.wait_recv()
        if stage == 0:
            lr_acc[...] += lr_rx[0]
        else:
            b = 3 * stage - 3
            lr_acc[...] += lr_rx[b + 1] + lr_rx[b + 2] + lr_rx[b + 3]

    h0 = ag_first(ad0, ad_hbm.at[:, pl.ds(0, 256)])
    ld_w += [load_w(g) for g in range(2, 8)]
    ld_x.wait()
    s0 = sib_part(0)
    matmul_half(0, 1)
    h1 = ag_first(ad1, ad_hbm.at[:, pl.ds(256, 256)])
    s1 = sib_part(1)
    matmul_half(1, 1)
    hu = ag_first(au0, au_hbm)
    ld_ad = load(ad_hbm, adv.at[z], lsem.at[1])
    ld_au = load(au_hbm, auv.at[z], lsem.at[2])
    ld_gs = load(g_hbm.at[:, cols(t)], gs, lsem.at[3])

    def rs_send(k):
        rs_tx[k] = (own[k] + sib_rx[k].astype(F32)).astype(BF)
        return send(rs_tx.at[k], rs_rx.at[k], at_p(OFFS[k]))

    s0.wait_recv()
    a0 = rs_send(0)
    s2 = sib_part(2)
    h0 = ag_next(ad0, h0, 2)
    matmul_half(2, 1)
    s1.wait_recv()
    a1 = rs_send(1)
    h1 = ag_next(ad1, h1, 2)
    s3 = sib_part(3)
    s2.wait_recv()
    a2 = rs_send(2)
    hu = ag_next(au0, hu, 2)
    lr_acc[...] = jnp.zeros_like(lr_acc)
    ld_ad.wait()
    ld_g = [load_g(g) for g in range(8)]
    project(0, z)
    h0 = ag_next(ad0, h0, 3)
    matmul_half(3, 1)
    project(0, slot(1))
    h1 = ag_next(ad1, h1, 3)
    ld_au.wait()
    ld_gs.wait()
    project(0, slot(7))
    project(1, z)
    project(0, slot(2))
    hu = ag_next(au0, hu, 3)
    project(0, slot(6))
    h0 = ag_next(ad0, h0, 4)
    s3.wait_recv()
    own[3] = own[3] + sib_rx[3].astype(F32)
    h1 = ag_next(ad1, h1, 4)
    project(1, slot(1))
    project(1, slot(7))
    project(0, slot(3))
    hu = ag_next(au0, hu, 4)
    project(0, slot(5))
    h0 = ag_next(ad0, h0, 5)
    project(1, slot(2))
    project(1, slot(6))
    h1 = ag_next(ad1, h1, 5)
    project(0, slot(4))
    project(1, slot(3))
    project(1, slot(5))
    hu = ag_next(au0, hu, 5)
    project(1, slot(4))
    lp = psum_start(0)
    a0.wait_recv()
    own[3] = own[3] + rs_rx[0].astype(F32)
    psum_end(0, lp)
    lp = psum_start(1)
    a1.wait_recv()
    a2.wait_recv()
    r_buf[...] = own[3] + (rs_rx[1].astype(F32) + rs_rx[2].astype(F32))
    p2 = []
    for k in (2, 1, 3):
        p2_tx[k - 1] = r_buf[:, cols(lax.rem(q + k, 4))].astype(BF)
        p2.append(send(p2_tx.at[k - 1], p2_rx.at[k - 1], at_q(k)))
    backward(0, 3, True)
    psum_end(1, lp)
    lp = psum_start(2)
    backward(3, 8, False)
    for cp in p2:
        cp.wait_recv()
    r_buf[:, 0:256] = (
        r_buf[:, cols(q)] + p2_rx[0].astype(F32) + p2_rx[1].astype(F32) + p2_rx[2].astype(F32)
    )
    psum_end(2, lp)

    def select(which):
        low = lr_acc[which].astype(BF).astype(F32)[None]
        for s in range(8):
            sel[which, pl.ds(s * 128, 128)] = (
                jnp.where(mask(s), low, 0.0).reshape(128, 256).astype(BF)
            )

    select(0)
    adapted = tn(sel[0], auv[...].reshape(1024, 256))
    fb[...] = (r_buf[:, 0:256] + adapted).astype(BF)

    def gather(block, device, rows=slice(None)):
        ref = mixed.at[rows, cols(block)]
        return send(ref, ref, device)

    mine = tid(p, q, c)
    own_out = mixed.at[:, cols(mine)]
    ag_p = {}
    ag_m = {}
    ag_q = {k: send(fb, own_out, at_q(k)) for k in (1, 3, 2)}
    sibs = []
    ld_own = load(fb, own_out, lsem.at[4])

    def grad_part(chain, s):
        rows = pl.ds(pl.multiple_of(s * 128, 128), 128)
        if chain == 0:
            return nn(sel[0, rows], gs[...])
        return nn(sel[1, rows], xv[:, (chain - 1) * 256:chain * 256])

    def rs_start(chain):
        zr_tx[chain, 0] = grad_part(chain, slot(4)).astype(BF)
        hp = send(zr_tx.at[chain, 0, TOP], zr_rx.at[chain, 0, TOP], zp)
        hm = send(zr_tx.at[chain, 0, LOW], zr_rx.at[chain, 0, LOW], zm)
        return hp, hm

    def rs_parts(chain, ks):
        for k in ks:
            zr_own[chain, 3 - k] = grad_part(chain, slot(k))
            zr_own[chain, 6 - k] = grad_part(chain, slot(-k))

    def rs_next(chain, step, prev):
        prev[0].wait_recv()
        if step == 1:
            zr_tx[chain, 1, TOP] = (zr_own[chain, 0, TOP] + zr_rx[chain, 0, TOP].astype(F32)).astype(BF)
            zr_tx[chain, 1, LOW] = zr_own[chain, 0, LOW].astype(BF)
        else:
            zr_tx[chain, step] = (zr_own[chain, step - 1] + zr_rx[chain, step - 1].astype(F32)).astype(BF)
        hp = send(zr_tx.at[chain, step], zr_rx.at[chain, step], zp)
        prev[1].wait_recv()
        if step == 1:
            zr_tx[chain, 4, TOP] = zr_own[chain, 3, TOP].astype(BF)
            zr_tx[chain, 4, LOW] = (zr_own[chain, 3, LOW] + zr_rx[chain, 0, LOW].astype(F32)).astype(BF)
        else:
            zr_tx[chain, 3 + step] = (
                zr_own[chain, 2 + step] + zr_rx[chain, 2 + step].astype(F32)
            ).astype(BF)
        hm = send(zr_tx.at[chain, 3 + step], zr_rx.at[chain, 3 + step], zm)
        return hp, hm

    def rs_end(chain, prev):
        prev[0].wait_recv()
        prev[1].wait_recv()
        return zr_own[chain, 6] + zr_rx[chain, 3].astype(F32) + zr_rx[chain, 6].astype(F32)

    def spread(k):
        ag_p[k].wait_recv()
        bm = tid(p + 3, q + k, c)
        f1 = gather(bm, at_p(1), pl.ds(0, 128))
        sibs.append(gather(bm, sib))
        ag_m[k].wait_recv()
        bq = tid(p + 1, q + k, c)
        f2 = gather(bq, at_p(3), pl.ds(128, 128))
        sibs.append(gather(bq, sib))
        return f1, f2

    def pass_on(k):
        ag_q[k].wait_recv()
        blk = tid(p, q + 4 - k, c)
        ag_p[4 - k] = gather(blk, at_p(1))
        ag_m[4 - k] = gather(blk, at_p(3))
        sibs.append(gather(blk, sib))

    def to_sib(k):
        for cp in halves[k]:
            cp.wait_recv()
        sibs.append(gather(tid(p + 2, q + k, c), sib))

    halves = {}
    cu = rs_start(0)
    select(1)
    ag_p[0] = send(fb, own_out, at_p(1))
    ag_m[0] = send(fb, own_out, at_p(3))
    sibs.append(send(fb, own_out, sib))
    c0 = rs_start(1)
    c1 = rs_start(2)
    for chain in range(3):
        rs_parts(chain, (3,))
    cu = rs_next(0, 1, cu)
    halves[0] = spread(0)
    c0 = rs_next(1, 1, c0)
    c1 = rs_next(2, 1, c1)
    pass_on(1)
    pass_on(3)
    pass_on(2)
    for chain in range(3):
        rs_parts(chain, (2,))
    hg_bf[...] = (hg_acc[...] + tn(sel[1], adv[...].reshape(1024, 512))).astype(BF)
    st_hg = load(hg_bf, hg_out, lsem.at[5])
    cu = rs_next(0, 2, cu)
    to_sib(0)
    c0 = rs_next(1, 2, c0)
    halves[3] = spread(3)
    c1 = rs_next(2, 2, c1)
    for chain in range(3):
        rs_parts(chain, (1,))
        zr_own[chain, 6] = grad_part(chain, z)
    halves[1] = spread(1)
    halves[2] = spread(2)
    cu = rs_next(0, 3, cu)
    c0 = rs_next(1, 3, c0)
    to_sib(3)
    c1 = rs_next(2, 3, c1)
    to_sib(1)
    to_sib(2)
    ug_buf[...] = rs_end(0, cu)
    st_ug = load(ug_buf, ug_out, lsem.at[6])
    for cp in sibs:
        cp.wait_recv()
    dg_buf[:, 0:256] = rs_end(1, c0)
    dg_buf[:, 256:512] = rs_end(2, c1)
    st_dg = load(dg_buf, dg_out, lsem.at[7])
    for cp in sent:
        cp.wait_send()
    for cp in (ld_own, st_hg, st_ug, st_dg):
        cp.wait()


def hand_over(*refs):
    sources, results, held, sems = refs[:4], refs[4:8], refs[8:12], refs[12]
    pieces = [(0, pl.ds(i * 32, 32)) for i in range(8)] + [(i, slice(None)) for i in (1, 2, 3)]
    inward = []
    for n, (i, rows) in enumerate(pieces):
        cp = pltpu.make_async_copy(sources[i].at[rows], held[i].at[rows], sems.at[0, n])
        cp.start()
        inward.append(cp)
    outward = []
    for n, (i, rows) in enumerate(pieces):
        inward[n].wait()
        cp = pltpu.make_async_copy(held[i].at[rows], results[i].at[rows], sems.at[1, n])
        cp.start()
        outward.append(cp)
    for cp in outward:
        cp.wait()


def on_device(x, g, ids, w, ad, au):
    any_spec = pl.BlockSpec(memory_space=pl.ANY)
    vmem = pl.BlockSpec(memory_space=pltpu.VMEM)
    shapes = (
        jax.ShapeDtypeStruct((256, 8192), BF),
        jax.ShapeDtypeStruct((256, 512), BF),
        jax.ShapeDtypeStruct((128, 512), F32),
        jax.ShapeDtypeStruct((128, 256), F32),
    )
    landed = pl.pallas_call(
        kernel,
        out_shape=shapes,
        in_specs=[any_spec, any_spec, vmem, any_spec, any_spec, any_spec],
        out_specs=(any_spec,) * 4,
        scratch_shapes=[
            pltpu.VMEM((256, 512), BF),
            pltpu.VMEM((256, 256), BF),
            pltpu.VMEM((8, 256, 1024), BF),
            pltpu.VMEM((8, 512, 1024), BF),
            pltpu.VMEM((8, 128, 512), BF),
            pltpu.VMEM((8, 128, 256), BF),
            pltpu.VMEM((4, 256, 1024), F32),
            pltpu.VMEM((4, 256, 1024), BF),
            pltpu.VMEM((4, 256, 1024), BF),
            pltpu.VMEM((3, 256, 1024), BF),
            pltpu.VMEM((3, 256, 1024), BF),
            pltpu.VMEM((256, 1024), F32),
            pltpu.VMEM((3, 256, 256), BF),
            pltpu.VMEM((3, 256, 256), BF),
            pltpu.VMEM((256, 256), BF),
            pltpu.VMEM((256, 512), F32),
            pltpu.VMEM((256, 512), BF),
            pltpu.VMEM((2, 16, 256), F32),
            pltpu.VMEM((3, 2, 16, 256), F32),
            pltpu.VMEM((7, 2, 16, 256), F32),
            pltpu.VMEM((2, 1024, 256), BF),
            pltpu.VMEM((3, 7, 128, 256), F32),
            pltpu.VMEM((3, 7, 128, 256), BF),
            pltpu.VMEM((3, 7, 128, 256), BF),
            pltpu.VMEM((128, 512), F32),
            pltpu.VMEM((128, 256), F32),
            pltpu.SemaphoreType.DMA((8,)),
            pltpu.SemaphoreType.DMA((32,)),
            pltpu.SemaphoreType.DMA((32,)),
            pltpu.SemaphoreType.DMA((NSEM,)),
            pltpu.SemaphoreType.DMA((NSEM,)),
        ],
        compiler_params=pltpu.CompilerParams(
            collective_id=0, has_side_effects=True, vmem_limit_bytes=56 * 2**20
        ),
    )(x, g, ids.reshape(1, 256), w, ad.reshape(128, 512), au.reshape(128, 256))
    mixed, hg, dg, ug = pl.pallas_call(
        hand_over,
        out_shape=shapes,
        in_specs=[any_spec] * 4,
        out_specs=(any_spec,) * 4,
        scratch_shapes=[pltpu.VMEM(one.shape, one.dtype) for one in shapes]
        + [pltpu.SemaphoreType.DMA((2, 11))],
        compiler_params=pltpu.CompilerParams(vmem_limit_bytes=60 * 2**20),
    )(*landed)
    return mixed, hg, dg.reshape(8, 16, 512), ug.reshape(8, 16, 256)


def solution(mesh):
    return jax.shard_map(
        on_device,
        mesh=mesh,
        in_specs=(
            P("adapter", "tensor"),
            P("adapter", None),
            P("adapter"),
            P("tensor", None),
            P("adapter", None, "tensor"),
            P("adapter", None, "tensor"),
        ),
        out_specs=(
            P("adapter", None),
            P("adapter", "tensor"),
            P("adapter", None, "tensor"),
            P("adapter", None, "tensor"),
        ),
        check_vma=False,
    )
```

```python
import jax
import jax.numpy as jnp
from jax import lax
from jax.experimental import pallas as pl
from jax.experimental.pallas import tpu as pltpu
from jax.sharding import PartitionSpec as P

BF = jnp.bfloat16
F32 = jnp.float32
MESH = pl.DeviceIdType.MESH
NSEM = 160
OFFS = (2, 1, 3, 0)


def nt(left, right):
    return lax.dot_general(left, right, (((1,), (1,)), ((), ())), preferred_element_type=F32)


def tn(left, right):
    return lax.dot_general(left, right, (((0,), (0,)), ((), ())), preferred_element_type=F32)


def nn(left, right):
    return lax.dot_general(left, right, (((1,), (0,)), ((), ())), preferred_element_type=F32)


def kernel(
    x_hbm, g_hbm, ids_ref, w_hbm, ad_hbm, au_hbm,
    mixed, hg_out, dg_out, ug_out,
    xv, gs, gv, wv, adv, auv,
    own, sib_tx, sib_rx, rs_tx, rs_rx, r_buf, p2_tx, p2_rx, gat,
    hg_acc, hg_bf, lr_acc, lr_tx, lr_rx, sel, zr_own, zr_tx, zr_rx, dg_buf, ug_buf,
    lsem, wsem, gsem, osem, ssem, rsem,
):
    z = lax.axis_index("adapter")
    t = lax.axis_index("tensor")
    c = lax.rem(t, 2)
    x = lax.rem(lax.div(t, 2), 4)
    y = lax.div(t, 8)
    d = 1 - c
    p = x * d + y * c
    q = y * d + x * c

    def tid(pp, qq, cc):
        return lax.rem(pp, 4) * (2 + 6 * cc) + lax.rem(qq, 4) * (8 - 6 * cc) + cc

    def cols(block):
        return pl.ds(pl.multiple_of(block * 256, 256), 256)

    sib = (z, t + 1 - 2 * c)

    def at_p(k):
        return (z, tid(p + k, q, c))

    def at_q(k):
        return (z, tid(p, q + k, c))

    def at_x(k):
        return (z, (y * 4 + lax.rem(x + k, 4)) * 2 + c)

    def at_y(k):
        return (z, (lax.rem(y + k, 4) * 4 + x) * 2 + c)

    zp = (lax.rem(z + 1, 8), t)
    zm = (lax.rem(z + 7, 8), t)

    def slot(k):
        return lax.rem(z + k + 8, 8)

    count = [0]
    sent = []

    def send(src, dst, device):
        i = count[0]
        count[0] += 1
        cp = pltpu.make_async_remote_copy(
            src_ref=src, dst_ref=dst, send_sem=ssem.at[i], recv_sem=rsem.at[i],
            device_id=device, device_id_type=MESH,
        )
        cp.start()
        sent.append(cp)
        return cp

    def load(src, dst, sem):
        cp = pltpu.make_async_copy(src, dst, sem)
        cp.start()
        return cp

    ld_x = load(x_hbm, xv, lsem.at[0])

    def group_block(g, j):
        k, mine = g // 2, g % 2
        if mine:
            return tid(p + OFFS[k], j, c)
        return tid(q + OFFS[k], j, d)

    def load_w(g):
        return [
            load(w_hbm.at[:, cols(group_block(g, j))], wv.at[g, :, pl.ds(j * 256, 256)], wsem.at[g * 4 + j])
            for j in range(4)
        ]

    def load_g(g):
        return [
            load(g_hbm.at[:, cols(group_block(g, j))], gv.at[g, :, pl.ds(j * 256, 256)], gsem.at[g * 4 + j])
            for j in range(4)
        ]

    ld_w = [load_w(0), load_w(1)]

    bar = pltpu.get_barrier_semaphore()
    for dev in [sib, zp, zm] + [at_x(k) for k in (1, 2, 3)] + [at_y(k) for k in (1, 2, 3)]:
        pl.semaphore_signal(bar, inc=1, device_id=dev, device_id_type=MESH)

    def matmul_half(k, mine):
        g = 2 * k + mine
        for cp in ld_w[g]:
            cp.wait()

        for j in range(2):
            at = pl.ds(j * 512, 512)
            res = nn(xv[...], wv[g, :, at])
            if mine:
                own[k, :, at] = res
            else:
                sib_tx[k, :, at] = res.astype(BF)

    pl.semaphore_wait(bar, 9)

    def ad0(s, rows=slice(None)):
        return adv.at[s, rows, pl.ds(0, 256)]

    def ad1(s, rows=slice(None)):
        return adv.at[s, rows, pl.ds(256, 256)]

    def au0(s, rows=slice(None)):
        return auv.at[s, rows, :]

    TOP, LOW = pl.ds(0, 64), pl.ds(64, 64)

    def ag_first(view, hbm):
        return send(hbm, view(z), zp), send(hbm, view(z), zm)

    def ag_next(view, prev, k):
        last = k == 4
        prev[0].wait_recv()
        if k < 5:
            ref = view(slot(1 - k), TOP) if last else view(slot(1 - k))
            hp = send(ref, ref, zp)
        prev[1].wait_recv()
        if k < 5:
            ref = view(slot(k - 1), LOW) if last else view(slot(k - 1))
            return hp, send(ref, ref, zm)
        return None

    def sib_part(k):
        matmul_half(k, 0)
        return send(sib_tx.at[k], sib_rx.at[k], sib)

    def mask(s):
        want = lax.broadcasted_iota(jnp.int32, (8, 1, 256), 0) + s * 8
        return want == ids_ref[...].reshape(1, 1, 256)

    def project(which, s):
        if which == 0:
            full = nt(adv[s], xv[...])
        else:
            full = nt(auv[s], gs[...])
        lr_acc[which] += jnp.sum(jnp.where(mask(s), full.reshape(8, 16, 256), 0.0), axis=0)

    def backward(lo, hi, first):
        for g in range(lo, hi):
            for cp in ld_g[g]:
                cp.wait()
        if first:
            hg_acc[...] = jnp.zeros_like(hg_acc)

        def body(g, carry):
            hg_acc[...] += nt(gv[g], wv[g])
            return carry

        lax.fori_loop(lo, hi, body, 0)

    def psum_start(which, stage):
        lr_tx[which, stage] = lr_acc[which]
        src = lr_tx.at[which, stage]
        if stage == 0:
            return [send(src, lr_rx.at[which, 0], sib)]
        at = at_x if stage == 1 else at_y
        return [send(src, lr_rx.at[which, 3 * stage - 3 + k], at(k)) for k in (2, 1, 3)]

    def psum_end(which, stage, cps):
        for cp in cps:
            cp.wait_recv()
        if stage == 0:
            lr_acc[which] += lr_rx[which, 0]
        else:
            b = 3 * stage - 3
            lr_acc[which] += lr_rx[which, b + 1] + lr_rx[which, b + 2] + lr_rx[which, b + 3]

    h0 = ag_first(ad0, ad_hbm.at[:, pl.ds(0, 256)])
    ld_w += [load_w(g) for g in range(2, 5)]
    h1 = ag_first(ad1, ad_hbm.at[:, pl.ds(256, 256)])
    ld_x.wait()
    s0 = sib_part(0)
    ld_w += [load_w(g) for g in range(5, 8)]
    hu = ag_first(au0, au_hbm)
    matmul_half(0, 1)
    s1 = sib_part(1)
    ld_ad = load(ad_hbm, adv.at[z], lsem.at[1])
    ld_au = load(au_hbm, auv.at[z], lsem.at[2])
    ld_gs = load(g_hbm.at[:, cols(t)], gs, lsem.at[3])

    def rs_send(k):
        rs_tx[k] = (own[k] + sib_rx[k].astype(F32)).astype(BF)
        return send(rs_tx.at[k], rs_rx.at[k], at_p(OFFS[k]))

    s0.wait_recv()
    a0 = rs_send(0)
    h0 = ag_next(ad0, h0, 2)
    matmul_half(1, 1)
    s2 = sib_part(2)
    h1 = ag_next(ad1, h1, 2)
    s1.wait_recv()
    a1 = rs_send(1)
    matmul_half(2, 1)
    hu = ag_next(au0, hu, 2)
    s2.wait_recv()
    a2 = rs_send(2)
    s3 = sib_part(3)
    h0 = ag_next(ad0, h0, 3)
    lr_acc[...] = jnp.zeros_like(lr_acc)
    ld_ad.wait()
    project(0, z)
    project(0, slot(1))
    project(0, slot(7))
    h1 = ag_next(ad1, h1, 3)
    matmul_half(3, 1)
    ld_g = [load_g(g) for g in range(8)]
    hu = ag_next(au0, hu, 3)
    project(0, slot(2))
    project(0, slot(6))
    h0 = ag_next(ad0, h0, 4)
    ld_au.wait()
    ld_gs.wait()
    project(1, z)
    project(1, slot(1))
    h1 = ag_next(ad1, h1, 4)
    project(0, slot(3))
    project(0, slot(5))
    hu = ag_next(au0, hu, 4)
    project(1, slot(7))
    project(1, slot(2))
    h0 = ag_next(ad0, h0, 5)
    s3.wait_recv()
    own[3] = own[3] + sib_rx[3].astype(F32)
    h1 = ag_next(ad1, h1, 5)
    project(0, slot(4))
    lp = psum_start(0, 0)
    project(1, slot(6))
    project(1, slot(3))
    project(1, slot(5))
    hu = ag_next(au0, hu, 5)
    psum_end(0, 0, lp)
    lp = psum_start(0, 1)
    project(1, slot(4))
    bp = psum_start(1, 0)
    a0.wait_recv()
    own[3] = own[3] + rs_rx[0].astype(F32)
    psum_end(1, 0, bp)
    bp = psum_start(1, 1)
    a1.wait_recv()
    a2.wait_recv()
    p2 = []
    for k in (2, 1, 3, 0):
        at = cols(lax.rem(q + k, 4))
        both = own[3, :, at] + (rs_rx[1, :, at].astype(F32) + rs_rx[2, :, at].astype(F32))
        if k:
            p2_tx[k - 1] = both.astype(BF)
            p2.append(send(p2_tx.at[k - 1], p2_rx.at[k - 1], at_q(k)))
        else:
            r_buf[...] = both
    psum_end(0, 1, lp)
    lp = psum_start(0, 2)
    backward(0, 3, True)
    psum_end(1, 1, bp)
    bp = psum_start(1, 2)
    backward(3, 6, False)
    for cp in p2:
        cp.wait_recv()
    r_buf[...] = r_buf[...] + p2_rx[0].astype(F32) + p2_rx[1].astype(F32) + p2_rx[2].astype(F32)
    psum_end(0, 2, lp)
    def select(which):
        low = lr_acc[which].astype(BF).astype(F32)[None]
        for s in range(8):
            sel[which, pl.ds(s * 128, 128)] = (
                jnp.where(mask(s), low, 0.0).reshape(128, 256).astype(BF)
            )

    select(0)
    adapted = tn(sel[0], auv[...].reshape(1024, 256))
    mine = tid(p, q, c)
    gat[mine] = (r_buf[...] + adapted).astype(BF)

    def gather(block, device, rows=slice(None)):
        ref = gat.at[block, rows]
        return send(ref, ref, device)

    outs = []

    def put_out(block):
        outs.append(load(gat.at[block], mixed.at[:, cols(block)], osem.at[len(outs)]))

    sibs = []

    def finish(a, b):
        block = tid(p + a, q + b, c)
        sibs.append((gather(block, sib), tid(q + a, p + b, d)))
        put_out(block)

    ag_p = {}
    ag_m = {}
    ag_q = {k: gather(mine, at_q(k)) for k in (1, 3, 2)}

    def grad_part(chain, s):
        rows = pl.ds(pl.multiple_of(s * 128, 128), 128)
        if chain == 0:
            return nn(sel[0, rows], gs[...])
        return nn(sel[1, rows], xv[:, (chain - 1) * 256:chain * 256])

    def rs_start(chain):
        zr_tx[chain, 0] = grad_part(chain, slot(4)).astype(BF)
        hp = send(zr_tx.at[chain, 0, TOP], zr_rx.at[chain, 0, TOP], zp)
        hm = send(zr_tx.at[chain, 0, LOW], zr_rx.at[chain, 0, LOW], zm)
        return hp, hm

    def rs_parts(chain, ks):
        for k in ks:
            zr_own[chain, 3 - k] = grad_part(chain, slot(k))
            zr_own[chain, 6 - k] = grad_part(chain, slot(-k))

    def rs_next(chain, step, prev):
        prev[0].wait_recv()
        if step == 1:
            zr_tx[chain, 1, TOP] = (zr_own[chain, 0, TOP] + zr_rx[chain, 0, TOP].astype(F32)).astype(BF)
            zr_tx[chain, 1, LOW] = zr_own[chain, 0, LOW].astype(BF)
        else:
            zr_tx[chain, step] = (zr_own[chain, step - 1] + zr_rx[chain, step - 1].astype(F32)).astype(BF)
        hp = send(zr_tx.at[chain, step], zr_rx.at[chain, step], zp)
        prev[1].wait_recv()
        if step == 1:
            zr_tx[chain, 4, TOP] = zr_own[chain, 3, TOP].astype(BF)
            zr_tx[chain, 4, LOW] = (zr_own[chain, 3, LOW] + zr_rx[chain, 0, LOW].astype(F32)).astype(BF)
        else:
            zr_tx[chain, 3 + step] = (
                zr_own[chain, 2 + step] + zr_rx[chain, 2 + step].astype(F32)
            ).astype(BF)
        hm = send(zr_tx.at[chain, 3 + step], zr_rx.at[chain, 3 + step], zm)
        return hp, hm

    def rs_end(chain, prev):
        prev[0].wait_recv()
        prev[1].wait_recv()
        return zr_own[chain, 6] + zr_rx[chain, 3].astype(F32) + zr_rx[chain, 6].astype(F32)

    def spread(k):
        ag_p[k].wait_recv()
        bm = tid(p + 3, q + k, c)
        f1 = gather(bm, at_p(1), pl.ds(0, 128))
        finish(3, k)
        ag_m[k].wait_recv()
        bq = tid(p + 1, q + k, c)
        f2 = gather(bq, at_p(3), pl.ds(128, 128))
        finish(1, k)
        return f1, f2

    def pass_on(k):
        ag_q[k].wait_recv()
        blk = tid(p, q + 4 - k, c)
        ag_p[4 - k] = gather(blk, at_p(1))
        ag_m[4 - k] = gather(blk, at_p(3))
        finish(0, 4 - k)

    def to_sib(k):
        for cp in halves[k]:
            cp.wait_recv()
        finish(2, k)

    halves = {}
    cu = rs_start(0)
    ag_p[0] = gather(mine, at_p(1))
    ag_m[0] = gather(mine, at_p(3))
    finish(0, 0)
    psum_end(1, 2, bp)
    select(1)
    c0 = rs_start(1)
    c1 = rs_start(2)
    for chain in range(3):
        rs_parts(chain, (3,))
    backward(6, 8, False)
    cu = rs_next(0, 1, cu)
    halves[0] = spread(0)
    c0 = rs_next(1, 1, c0)
    c1 = rs_next(2, 1, c1)
    pass_on(1)
    pass_on(3)
    pass_on(2)
    for chain in range(3):
        rs_parts(chain, (2,))
    hg_bf[...] = (hg_acc[...] + tn(sel[1], adv[...].reshape(1024, 512))).astype(BF)
    st_hg = load(hg_bf, hg_out, lsem.at[5])
    cu = rs_next(0, 2, cu)
    to_sib(0)
    c0 = rs_next(1, 2, c0)
    halves[3] = spread(3)
    c1 = rs_next(2, 2, c1)
    for chain in range(3):
        rs_parts(chain, (1,))
        zr_own[chain, 6] = grad_part(chain, z)
    halves[1] = spread(1)
    halves[2] = spread(2)
    cu = rs_next(0, 3, cu)
    c0 = rs_next(1, 3, c0)
    to_sib(3)
    c1 = rs_next(2, 3, c1)
    to_sib(1)
    to_sib(2)
    ug_buf[...] = rs_end(0, cu)
    st_ug = load(ug_buf, ug_out, lsem.at[6])
    for cp, block in sibs:
        cp.wait_recv()
        put_out(block)
    dg_buf[:, 0:256] = rs_end(1, c0)
    dg_buf[:, 256:512] = rs_end(2, c1)
    st_dg = load(dg_buf, dg_out, lsem.at[7])
    for cp in sent:
        cp.wait_send()
    for cp in outs + [st_hg, st_ug, st_dg]:
        cp.wait()


def hand_over(*refs):
    sources, results, held, sems = refs[:4], refs[4:8], refs[8:12], refs[12]
    pieces = [(0, pl.ds(i * 32, 32)) for i in range(8)] + [(i, slice(None)) for i in (1, 2, 3)]
    inward = []
    for n, (i, rows) in enumerate(pieces):
        cp = pltpu.make_async_copy(sources[i].at[rows], held[i].at[rows], sems.at[0, n])
        cp.start()
        inward.append(cp)
    outward = []
    for n, (i, rows) in enumerate(pieces):
        inward[n].wait()
        cp = pltpu.make_async_copy(held[i].at[rows], results[i].at[rows], sems.at[1, n])
        cp.start()
        outward.append(cp)
    for cp in outward:
        cp.wait()


def on_device(x, g, ids, w, ad, au):
    any_spec = pl.BlockSpec(memory_space=pl.ANY)
    vmem = pl.BlockSpec(memory_space=pltpu.VMEM)
    shapes = (
        jax.ShapeDtypeStruct((256, 8192), BF),
        jax.ShapeDtypeStruct((256, 512), BF),
        jax.ShapeDtypeStruct((128, 512), F32),
        jax.ShapeDtypeStruct((128, 256), F32),
    )
    landed = pl.pallas_call(
        kernel,
        out_shape=shapes,
        in_specs=[any_spec, any_spec, vmem, any_spec, any_spec, any_spec],
        out_specs=(any_spec,) * 4,
        scratch_shapes=[
            pltpu.VMEM((256, 512), BF),
            pltpu.VMEM((256, 256), BF),
            pltpu.VMEM((8, 256, 1024), BF),
            pltpu.VMEM((8, 512, 1024), BF),
            pltpu.VMEM((8, 128, 512), BF),
            pltpu.VMEM((8, 128, 256), BF),
            pltpu.VMEM((4, 256, 1024), F32),
            pltpu.VMEM((4, 256, 1024), BF),
            pltpu.VMEM((4, 256, 1024), BF),
            pltpu.VMEM((3, 256, 1024), BF),
            pltpu.VMEM((3, 256, 1024), BF),
            pltpu.VMEM((256, 256), F32),
            pltpu.VMEM((3, 256, 256), BF),
            pltpu.VMEM((3, 256, 256), BF),
            pltpu.VMEM((32, 256, 256), BF),
            pltpu.VMEM((256, 512), F32),
            pltpu.VMEM((256, 512), BF),
            pltpu.VMEM((2, 16, 256), F32),
            pltpu.VMEM((2, 3, 16, 256), F32),
            pltpu.VMEM((2, 7, 16, 256), F32),
            pltpu.VMEM((2, 1024, 256), BF),
            pltpu.VMEM((3, 7, 128, 256), F32),
            pltpu.VMEM((3, 7, 128, 256), BF),
            pltpu.VMEM((3, 7, 128, 256), BF),
            pltpu.VMEM((128, 512), F32),
            pltpu.VMEM((128, 256), F32),
            pltpu.SemaphoreType.DMA((8,)),
            pltpu.SemaphoreType.DMA((32,)),
            pltpu.SemaphoreType.DMA((32,)),
            pltpu.SemaphoreType.DMA((32,)),
            pltpu.SemaphoreType.DMA((NSEM,)),
            pltpu.SemaphoreType.DMA((NSEM,)),
        ],
        compiler_params=pltpu.CompilerParams(
            collective_id=0, has_side_effects=True, vmem_limit_bytes=56 * 2**20
        ),
    )(x, g, ids.reshape(1, 256), w, ad.reshape(128, 512), au.reshape(128, 256))
    mixed, hg, dg, ug = pl.pallas_call(
        hand_over,
        out_shape=shapes,
        in_specs=[any_spec] * 4,
        out_specs=(any_spec,) * 4,
        scratch_shapes=[pltpu.VMEM(one.shape, one.dtype) for one in shapes]
        + [pltpu.SemaphoreType.DMA((2, 11))],
        compiler_params=pltpu.CompilerParams(vmem_limit_bytes=60 * 2**20),
    )(*landed)
    return mixed, hg, dg.reshape(8, 16, 512), ug.reshape(8, 16, 256)


def solution(mesh):
    return jax.shard_map(
        on_device,
        mesh=mesh,
        in_specs=(
            P("adapter", "tensor"),
            P("adapter", None),
            P("adapter"),
            P("tensor", None),
            P("adapter", None, "tensor"),
            P("adapter", None, "tensor"),
        ),
        out_specs=(
            P("adapter", None),
            P("adapter", "tensor"),
            P("adapter", None, "tensor"),
            P("adapter", None, "tensor"),
        ),
        check_vma=False,
    )
```

```python
import jax
import jax.numpy as jnp
from jax import lax
from jax.experimental import pallas as pl
from jax.experimental.pallas import tpu as pltpu
from jax.sharding import PartitionSpec as P

BF = jnp.bfloat16
F32 = jnp.float32
MESH = pl.DeviceIdType.MESH
NSEM = 160
OFFS = (2, 1, 3, 0)


def nt(left, right):
    return lax.dot_general(left, right, (((1,), (1,)), ((), ())), preferred_element_type=F32)


def tn(left, right):
    return lax.dot_general(left, right, (((0,), (0,)), ((), ())), preferred_element_type=F32)


def nn(left, right):
    return lax.dot_general(left, right, (((1,), (0,)), ((), ())), preferred_element_type=F32)


def kernel(
    x_hbm, g_hbm, ids_ref, w_hbm, ad_hbm, au_hbm,
    mixed, hg_out, dg_out, ug_out,
    xv, gs, gv, wv, adv, auv,
    own, sib_tx, sib_rx, rs_tx, rs_rx, r_buf, p2_tx, p2_rx, gat,
    hg_acc, hg_bf, lr_acc, lr_tx, lr_rx, sel, zr_own, zr_tx, zr_rx, dg_buf, ug_buf,
    lsem, wsem, gsem, osem, ssem, rsem,
):
    z = lax.axis_index("adapter")
    t = lax.axis_index("tensor")
    c = lax.rem(t, 2)
    x = lax.rem(lax.div(t, 2), 4)
    y = lax.div(t, 8)
    d = 1 - c
    p = x * d + y * c
    q = y * d + x * c

    def tid(pp, qq, cc):
        return lax.rem(pp, 4) * (2 + 6 * cc) + lax.rem(qq, 4) * (8 - 6 * cc) + cc

    def cols(block):
        return pl.ds(pl.multiple_of(block * 256, 256), 256)

    sib = (z, t + 1 - 2 * c)

    def at_p(k):
        return (z, tid(p + k, q, c))

    def at_q(k):
        return (z, tid(p, q + k, c))

    def at_x(k):
        return (z, (y * 4 + lax.rem(x + k, 4)) * 2 + c)

    def at_y(k):
        return (z, (lax.rem(y + k, 4) * 4 + x) * 2 + c)

    zp = (lax.rem(z + 1, 8), t)
    zm = (lax.rem(z + 7, 8), t)

    def slot(k):
        return lax.rem(z + k + 8, 8)

    count = [0]
    sent = []

    def send(src, dst, device):
        i = count[0]
        count[0] += 1
        cp = pltpu.make_async_remote_copy(
            src_ref=src, dst_ref=dst, send_sem=ssem.at[i], recv_sem=rsem.at[i],
            device_id=device, device_id_type=MESH,
        )
        cp.start()
        sent.append(cp)
        return cp

    def load(src, dst, sem):
        cp = pltpu.make_async_copy(src, dst, sem)
        cp.start()
        return cp

    ld_x = load(x_hbm, xv, lsem.at[0])

    def group_block(g, j):
        k, mine = g // 2, g % 2
        if mine:
            return tid(p + OFFS[k], j, c)
        return tid(q + OFFS[k], j, d)

    def load_w(g):
        return [
            load(w_hbm.at[:, cols(group_block(g, j))], wv.at[g, :, pl.ds(j * 256, 256)], wsem.at[g * 4 + j])
            for j in range(4)
        ]

    def load_g(g):
        return [
            load(g_hbm.at[:, cols(group_block(g, j))], gv.at[g, :, pl.ds(j * 256, 256)], gsem.at[g * 4 + j])
            for j in range(4)
        ]

    ld_w = [load_w(0), load_w(1)]

    bar = pltpu.get_barrier_semaphore()
    for dev in [sib, zp, zm] + [at_x(k) for k in (1, 2, 3)] + [at_y(k) for k in (1, 2, 3)]:
        pl.semaphore_signal(bar, inc=1, device_id=dev, device_id_type=MESH)

    def matmul_half(k, mine):
        g = 2 * k + mine
        for cp in ld_w[g]:
            cp.wait()

        for j in range(2):
            at = pl.ds(j * 512, 512)
            res = nn(xv[...], wv[g, :, at])
            if mine:
                own[k, :, at] = res
            else:
                sib_tx[k, :, at] = res.astype(BF)

    pl.semaphore_wait(bar, 9)

    def ad0(s, rows=slice(None)):
        return adv.at[s, rows, pl.ds(0, 256)]

    def ad1(s, rows=slice(None)):
        return adv.at[s, rows, pl.ds(256, 256)]

    def au0(s, rows=slice(None)):
        return auv.at[s, rows, :]

    TOP, LOW = pl.ds(0, 64), pl.ds(64, 64)

    def ag_first(view, hbm):
        return send(hbm, view(z), zp), send(hbm, view(z), zm)

    def ag_next(view, prev, k):
        last = k == 4
        prev[0].wait_recv()
        if k < 5:
            ref = view(slot(1 - k), TOP) if last else view(slot(1 - k))
            hp = send(ref, ref, zp)
        prev[1].wait_recv()
        if k < 5:
            ref = view(slot(k - 1), LOW) if last else view(slot(k - 1))
            return hp, send(ref, ref, zm)
        return None

    def sib_part(k):
        matmul_half(k, 0)
        return send(sib_tx.at[k], sib_rx.at[k], sib)

    def mask(s):
        want = lax.broadcasted_iota(jnp.int32, (8, 1, 256), 0) + s * 8
        return want == ids_ref[...].reshape(1, 1, 256)

    def project(which, s):
        if which == 0:
            full = nt(adv[s], xv[...])
        else:
            full = nt(auv[s], gs[...])
        lr_acc[which] += jnp.sum(jnp.where(mask(s), full.reshape(8, 16, 256), 0.0), axis=0)

    def backward(lo, hi, first):
        for g in range(lo, hi):
            for cp in ld_g[g]:
                cp.wait()
        if first:
            hg_acc[...] = jnp.zeros_like(hg_acc)

        def body(g, carry):
            hg_acc[...] += nt(gv[g], wv[g])
            return carry

        lax.fori_loop(lo, hi, body, 0)

    def psum_start(which, stage):
        lr_tx[which, stage] = lr_acc[which]
        src = lr_tx.at[which, stage]
        if stage == 0:
            return [send(src, lr_rx.at[which, 0], sib)]
        at = at_x if stage == 1 else at_y
        return [send(src, lr_rx.at[which, 3 * stage - 3 + k], at(k)) for k in (2, 1, 3)]

    def psum_end(which, stage, cps):
        for cp in cps:
            cp.wait_recv()
        if stage == 0:
            lr_acc[which] += lr_rx[which, 0]
        else:
            b = 3 * stage - 3
            lr_acc[which] += lr_rx[which, b + 1] + lr_rx[which, b + 2] + lr_rx[which, b + 3]

    h0 = ag_first(ad0, ad_hbm.at[:, pl.ds(0, 256)])
    ld_w += [load_w(g) for g in range(2, 5)]
    h1 = ag_first(ad1, ad_hbm.at[:, pl.ds(256, 256)])
    ld_x.wait()
    s0 = sib_part(0)
    ld_w += [load_w(g) for g in range(5, 8)]
    hu = ag_first(au0, au_hbm)
    matmul_half(0, 1)
    s1 = sib_part(1)
    ld_ad = load(ad_hbm, adv.at[z], lsem.at[1])
    ld_au = load(au_hbm, auv.at[z], lsem.at[2])
    ld_gs = load(g_hbm.at[:, cols(t)], gs, lsem.at[3])

    def rs_send(k):
        rs_tx[k] = (own[k] + sib_rx[k].astype(F32)).astype(BF)
        return send(rs_tx.at[k], rs_rx.at[k], at_p(OFFS[k]))

    s0.wait_recv()
    a0 = rs_send(0)
    h0 = ag_next(ad0, h0, 2)
    matmul_half(1, 1)
    s2 = sib_part(2)
    h1 = ag_next(ad1, h1, 2)
    s1.wait_recv()
    a1 = rs_send(1)
    matmul_half(2, 1)
    hu = ag_next(au0, hu, 2)
    s2.wait_recv()
    a2 = rs_send(2)
    s3 = sib_part(3)
    h0 = ag_next(ad0, h0, 3)
    lr_acc[...] = jnp.zeros_like(lr_acc)
    ld_ad.wait()
    project(0, z)
    project(0, slot(1))
    project(0, slot(7))
    h1 = ag_next(ad1, h1, 3)
    matmul_half(3, 1)
    ld_g = [load_g(g) for g in range(8)]
    hu = ag_next(au0, hu, 3)
    project(0, slot(2))
    project(0, slot(6))
    h0 = ag_next(ad0, h0, 4)
    ld_au.wait()
    ld_gs.wait()
    project(1, z)
    project(1, slot(1))
    h1 = ag_next(ad1, h1, 4)
    project(0, slot(3))
    project(0, slot(5))
    hu = ag_next(au0, hu, 4)
    project(1, slot(7))
    project(1, slot(2))
    h0 = ag_next(ad0, h0, 5)
    s3.wait_recv()
    own[3] = own[3] + sib_rx[3].astype(F32)
    h1 = ag_next(ad1, h1, 5)
    project(0, slot(4))
    lp = psum_start(0, 0)
    project(1, slot(6))
    project(1, slot(3))
    project(1, slot(5))
    hu = ag_next(au0, hu, 5)
    psum_end(0, 0, lp)
    lp = psum_start(0, 1)
    project(1, slot(4))
    bp = psum_start(1, 0)
    a0.wait_recv()
    own[3] = own[3] + rs_rx[0].astype(F32)
    psum_end(1, 0, bp)
    bp = psum_start(1, 1)
    a1.wait_recv()
    a2.wait_recv()
    p2 = []
    for k in (2, 1, 3, 0):
        at = cols(lax.rem(q + k, 4))
        both = own[3, :, at] + (rs_rx[1, :, at].astype(F32) + rs_rx[2, :, at].astype(F32))
        if k:
            p2_tx[k - 1] = both.astype(BF)
            p2.append(send(p2_tx.at[k - 1], p2_rx.at[k - 1], at_q(k)))
        else:
            r_buf[...] = both
    psum_end(0, 1, lp)
    lp = psum_start(0, 2)
    backward(0, 3, True)
    psum_end(1, 1, bp)
    bp = psum_start(1, 2)
    backward(3, 6, False)
    for cp in p2:
        cp.wait_recv()
    r_buf[...] = r_buf[...] + p2_rx[0].astype(F32) + p2_rx[1].astype(F32) + p2_rx[2].astype(F32)
    psum_end(0, 2, lp)
    def select(which):
        low = lr_acc[which].astype(BF).astype(F32)[None]
        for s in range(8):
            sel[which, pl.ds(s * 128, 128)] = (
                jnp.where(mask(s), low, 0.0).reshape(128, 256).astype(BF)
            )

    select(0)
    adapted = tn(sel[0], auv[...].reshape(1024, 256))
    mine = tid(p, q, c)
    gat[mine] = (r_buf[...] + adapted).astype(BF)

    def gather(block, device, rows=slice(None)):
        ref = gat.at[block, rows]
        return send(ref, ref, device)

    outs = []

    def put_out(block):
        outs.append(load(gat.at[block], mixed.at[:, cols(block)], osem.at[len(outs)]))

    sibs = []

    def finish(a, b):
        block = tid(p + a, q + b, c)
        sibs.append((gather(block, sib), tid(q + a, p + b, d)))
        put_out(block)

    ag_p = {}
    ag_m = {}
    ag_q = {k: gather(mine, at_q(k)) for k in (2, 1, 3)}

    def grad_part(chain, s):
        rows = pl.ds(pl.multiple_of(s * 128, 128), 128)
        if chain == 0:
            return nn(sel[0, rows], gs[...])
        return nn(sel[1, rows], xv[:, (chain - 1) * 256:chain * 256])

    def rs_start(chain):
        zr_tx[chain, 0] = grad_part(chain, slot(4)).astype(BF)
        hp = send(zr_tx.at[chain, 0, TOP], zr_rx.at[chain, 0, TOP], zp)
        hm = send(zr_tx.at[chain, 0, LOW], zr_rx.at[chain, 0, LOW], zm)
        return hp, hm

    def rs_parts(chain, ks):
        for k in ks:
            zr_own[chain, 3 - k] = grad_part(chain, slot(k))
            zr_own[chain, 6 - k] = grad_part(chain, slot(-k))

    def rs_next(chain, step, prev):
        prev[0].wait_recv()
        if step == 1:
            zr_tx[chain, 1, TOP] = (zr_own[chain, 0, TOP] + zr_rx[chain, 0, TOP].astype(F32)).astype(BF)
            zr_tx[chain, 1, LOW] = zr_own[chain, 0, LOW].astype(BF)
        else:
            zr_tx[chain, step] = (zr_own[chain, step - 1] + zr_rx[chain, step - 1].astype(F32)).astype(BF)
        hp = send(zr_tx.at[chain, step], zr_rx.at[chain, step], zp)
        prev[1].wait_recv()
        if step == 1:
            zr_tx[chain, 4, TOP] = zr_own[chain, 3, TOP].astype(BF)
            zr_tx[chain, 4, LOW] = (zr_own[chain, 3, LOW] + zr_rx[chain, 0, LOW].astype(F32)).astype(BF)
        else:
            zr_tx[chain, 3 + step] = (
                zr_own[chain, 2 + step] + zr_rx[chain, 2 + step].astype(F32)
            ).astype(BF)
        hm = send(zr_tx.at[chain, 3 + step], zr_rx.at[chain, 3 + step], zm)
        return hp, hm

    def rs_end(chain, prev):
        prev[0].wait_recv()
        prev[1].wait_recv()
        return zr_own[chain, 6] + zr_rx[chain, 3].astype(F32) + zr_rx[chain, 6].astype(F32)

    def spread(k):
        ag_p[k].wait_recv()
        bm = tid(p + 3, q + k, c)
        f1 = gather(bm, at_p(1), pl.ds(0, 128))
        finish(3, k)
        ag_m[k].wait_recv()
        bq = tid(p + 1, q + k, c)
        f2 = gather(bq, at_p(3), pl.ds(128, 128))
        finish(1, k)
        return f1, f2

    def pass_on(k):
        ag_q[k].wait_recv()
        blk = tid(p, q + 4 - k, c)
        ag_p[4 - k] = gather(blk, at_p(1))
        ag_m[4 - k] = gather(blk, at_p(3))
        finish(0, 4 - k)

    def to_sib(k):
        for cp in halves[k]:
            cp.wait_recv()
        finish(2, k)

    halves = {}
    cu = rs_start(0)
    finish(0, 0)
    psum_end(1, 2, bp)
    select(1)
    c0 = rs_start(1)
    c1 = rs_start(2)
    for chain in range(3):
        rs_parts(chain, (3,))
    ag_p[0] = gather(mine, at_p(1))
    ag_m[0] = gather(mine, at_p(3))
    backward(6, 8, False)
    cu = rs_next(0, 1, cu)
    pass_on(1)
    pass_on(3)
    pass_on(2)
    c0 = rs_next(1, 1, c0)
    c1 = rs_next(2, 1, c1)
    halves[0] = spread(0)
    for chain in range(3):
        rs_parts(chain, (2,))
    hg_bf[...] = (hg_acc[...] + tn(sel[1], adv[...].reshape(1024, 512))).astype(BF)
    st_hg = load(hg_bf, hg_out, lsem.at[5])
    cu = rs_next(0, 2, cu)
    to_sib(0)
    c0 = rs_next(1, 2, c0)
    halves[3] = spread(3)
    c1 = rs_next(2, 2, c1)
    for chain in range(3):
        rs_parts(chain, (1,))
        zr_own[chain, 6] = grad_part(chain, z)
    halves[1] = spread(1)
    halves[2] = spread(2)
    cu = rs_next(0, 3, cu)
    c0 = rs_next(1, 3, c0)
    to_sib(3)
    c1 = rs_next(2, 3, c1)
    to_sib(1)
    to_sib(2)
    ug_buf[...] = rs_end(0, cu)
    st_ug = load(ug_buf, ug_out, lsem.at[6])
    for cp, block in sibs:
        cp.wait_recv()
        put_out(block)
    dg_buf[:, 0:256] = rs_end(1, c0)
    dg_buf[:, 256:512] = rs_end(2, c1)
    st_dg = load(dg_buf, dg_out, lsem.at[7])
    for cp in sent:
        cp.wait_send()
    for cp in outs + [st_hg, st_ug, st_dg]:
        cp.wait()


def hand_over(*refs):
    sources, results, held, sems = refs[:4], refs[4:8], refs[8:12], refs[12]
    pieces = [(0, pl.ds(i * 32, 32)) for i in range(8)] + [(i, slice(None)) for i in (1, 2, 3)]
    inward = []
    for n, (i, rows) in enumerate(pieces):
        cp = pltpu.make_async_copy(sources[i].at[rows], held[i].at[rows], sems.at[0, n])
        cp.start()
        inward.append(cp)
    outward = []
    for n, (i, rows) in enumerate(pieces):
        inward[n].wait()
        cp = pltpu.make_async_copy(held[i].at[rows], results[i].at[rows], sems.at[1, n])
        cp.start()
        outward.append(cp)
    for cp in outward:
        cp.wait()


def on_device(x, g, ids, w, ad, au):
    any_spec = pl.BlockSpec(memory_space=pl.ANY)
    vmem = pl.BlockSpec(memory_space=pltpu.VMEM)
    shapes = (
        jax.ShapeDtypeStruct((256, 8192), BF),
        jax.ShapeDtypeStruct((256, 512), BF),
        jax.ShapeDtypeStruct((128, 512), F32),
        jax.ShapeDtypeStruct((128, 256), F32),
    )
    landed = pl.pallas_call(
        kernel,
        out_shape=shapes,
        in_specs=[any_spec, any_spec, vmem, any_spec, any_spec, any_spec],
        out_specs=(any_spec,) * 4,
        scratch_shapes=[
            pltpu.VMEM((256, 512), BF),
            pltpu.VMEM((256, 256), BF),
            pltpu.VMEM((8, 256, 1024), BF),
            pltpu.VMEM((8, 512, 1024), BF),
            pltpu.VMEM((8, 128, 512), BF),
            pltpu.VMEM((8, 128, 256), BF),
            pltpu.VMEM((4, 256, 1024), F32),
            pltpu.VMEM((4, 256, 1024), BF),
            pltpu.VMEM((4, 256, 1024), BF),
            pltpu.VMEM((3, 256, 1024), BF),
            pltpu.VMEM((3, 256, 1024), BF),
            pltpu.VMEM((256, 256), F32),
            pltpu.VMEM((3, 256, 256), BF),
            pltpu.VMEM((3, 256, 256), BF),
            pltpu.VMEM((32, 256, 256), BF),
            pltpu.VMEM((256, 512), F32),
            pltpu.VMEM((256, 512), BF),
            pltpu.VMEM((2, 16, 256), F32),
            pltpu.VMEM((2, 3, 16, 256), F32),
            pltpu.VMEM((2, 7, 16, 256), F32),
            pltpu.VMEM((2, 1024, 256), BF),
            pltpu.VMEM((3, 7, 128, 256), F32),
            pltpu.VMEM((3, 7, 128, 256), BF),
            pltpu.VMEM((3, 7, 128, 256), BF),
            pltpu.VMEM((128, 512), F32),
            pltpu.VMEM((128, 256), F32),
            pltpu.SemaphoreType.DMA((8,)),
            pltpu.SemaphoreType.DMA((32,)),
            pltpu.SemaphoreType.DMA((32,)),
            pltpu.SemaphoreType.DMA((32,)),
            pltpu.SemaphoreType.DMA((NSEM,)),
            pltpu.SemaphoreType.DMA((NSEM,)),
        ],
        compiler_params=pltpu.CompilerParams(
            collective_id=0, has_side_effects=True, vmem_limit_bytes=56 * 2**20
        ),
    )(x, g, ids.reshape(1, 256), w, ad.reshape(128, 512), au.reshape(128, 256))
    mixed, hg, dg, ug = pl.pallas_call(
        hand_over,
        out_shape=shapes,
        in_specs=[any_spec] * 4,
        out_specs=(any_spec,) * 4,
        scratch_shapes=[pltpu.VMEM(one.shape, one.dtype) for one in shapes]
        + [pltpu.SemaphoreType.DMA((2, 11))],
        compiler_params=pltpu.CompilerParams(vmem_limit_bytes=60 * 2**20),
    )(*landed)
    return mixed, hg, dg.reshape(8, 16, 512), ug.reshape(8, 16, 256)


def solution(mesh):
    return jax.shard_map(
        on_device,
        mesh=mesh,
        in_specs=(
            P("adapter", "tensor"),
            P("adapter", None),
            P("adapter"),
            P("tensor", None),
            P("adapter", None, "tensor"),
            P("adapter", None, "tensor"),
        ),
        out_specs=(
            P("adapter", None),
            P("adapter", "tensor"),
            P("adapter", None, "tensor"),
            P("adapter", None, "tensor"),
        ),
        check_vma=False,
    )
```

```python
import jax
import jax.numpy as jnp
from jax import lax
from jax.experimental import pallas as pl
from jax.experimental.pallas import tpu as pltpu
from jax.sharding import PartitionSpec as P

BF = jnp.bfloat16
F32 = jnp.float32
MESH = pl.DeviceIdType.MESH
NSEM = 160
OFFS = (2, 1, 3, 0)


def nt(left, right):
    return lax.dot_general(left, right, (((1,), (1,)), ((), ())), preferred_element_type=F32)


def tn(left, right):
    return lax.dot_general(left, right, (((0,), (0,)), ((), ())), preferred_element_type=F32)


def nn(left, right):
    return lax.dot_general(left, right, (((1,), (0,)), ((), ())), preferred_element_type=F32)


def kernel(
    x_hbm, g_hbm, ids_ref, w_hbm, ad_hbm, au_hbm,
    mixed, hg_out, dg_out, ug_out,
    xv, gs, gv, wv, adv, auv,
    own, sib_tx, sib_rx, rs_tx, rs_rx, r_buf, p2_tx, p2_rx, gat,
    hg_acc, hg_bf, lr_acc, lr_tx, lr_rx, sel, zr_own, zr_tx, zr_rx, dg_buf, ug_buf,
    lsem, wsem, gsem, osem, ssem, rsem,
):
    z = lax.axis_index("adapter")
    t = lax.axis_index("tensor")
    c = lax.rem(t, 2)
    x = lax.rem(lax.div(t, 2), 4)
    y = lax.div(t, 8)
    d = 1 - c
    p = x * d + y * c
    q = y * d + x * c

    def tid(pp, qq, cc):
        return lax.rem(pp, 4) * (2 + 6 * cc) + lax.rem(qq, 4) * (8 - 6 * cc) + cc

    def cols(block):
        return pl.ds(pl.multiple_of(block * 256, 256), 256)

    sib = (z, t + 1 - 2 * c)

    def at_p(k):
        return (z, tid(p + k, q, c))

    def at_q(k):
        return (z, tid(p, q + k, c))

    def at_x(k):
        return (z, (y * 4 + lax.rem(x + k, 4)) * 2 + c)

    def at_y(k):
        return (z, (lax.rem(y + k, 4) * 4 + x) * 2 + c)

    zp = (lax.rem(z + 1, 8), t)
    zm = (lax.rem(z + 7, 8), t)

    def slot(k):
        return lax.rem(z + k + 8, 8)

    count = [0]
    sent = []

    def send(src, dst, device):
        i = count[0]
        count[0] += 1
        cp = pltpu.make_async_remote_copy(
            src_ref=src, dst_ref=dst, send_sem=ssem.at[i], recv_sem=rsem.at[i],
            device_id=device, device_id_type=MESH,
        )
        cp.start()
        sent.append(cp)
        return cp

    def load(src, dst, sem):
        cp = pltpu.make_async_copy(src, dst, sem)
        cp.start()
        return cp

    ld_x = load(x_hbm, xv, lsem.at[0])

    def group_block(g, j):
        k, mine = g // 2, g % 2
        if mine:
            return tid(p + OFFS[k], j, c)
        return tid(q + OFFS[k], j, d)

    def load_w(g):
        return [
            load(w_hbm.at[:, cols(group_block(g, j))], wv.at[g, :, pl.ds(j * 256, 256)], wsem.at[g * 4 + j])
            for j in range(4)
        ]

    def load_g(g):
        return [
            load(g_hbm.at[:, cols(group_block(g, j))], gv.at[g, :, pl.ds(j * 256, 256)], gsem.at[g * 4 + j])
            for j in range(4)
        ]

    ld_w = [load_w(0), load_w(1)]

    bar = pltpu.get_barrier_semaphore()
    for dev in [sib, zp, zm] + [at_x(k) for k in (1, 2, 3)] + [at_y(k) for k in (1, 2, 3)]:
        pl.semaphore_signal(bar, inc=1, device_id=dev, device_id_type=MESH)

    def matmul_half(k, mine):
        g = 2 * k + mine
        for cp in ld_w[g]:
            cp.wait()

        for j in range(2):
            at = pl.ds(j * 512, 512)
            res = nn(xv[...], wv[g, :, at])
            if mine:
                own[k, :, at] = res
            else:
                sib_tx[k, :, at] = res.astype(BF)

    pl.semaphore_wait(bar, 9)

    def ad0(s, rows=slice(None)):
        return adv.at[s, rows, pl.ds(0, 256)]

    def ad1(s, rows=slice(None)):
        return adv.at[s, rows, pl.ds(256, 256)]

    def au0(s, rows=slice(None)):
        return auv.at[s, rows, :]

    TOP, LOW = pl.ds(0, 64), pl.ds(64, 64)

    def ag_first(view, hbm):
        return send(hbm, view(z), zp), send(hbm, view(z), zm)

    def ag_next(view, prev, k):
        last = k == 4
        prev[0].wait_recv()
        if k < 5:
            ref = view(slot(1 - k), TOP) if last else view(slot(1 - k))
            hp = send(ref, ref, zp)
        prev[1].wait_recv()
        if k < 5:
            ref = view(slot(k - 1), LOW) if last else view(slot(k - 1))
            return hp, send(ref, ref, zm)
        return None

    def sib_part(k):
        matmul_half(k, 0)
        return send(sib_tx.at[k], sib_rx.at[k], sib)

    def mask(s):
        want = lax.broadcasted_iota(jnp.int32, (8, 1, 256), 0) + s * 8
        return want == ids_ref[...].reshape(1, 1, 256)

    def project(which, s):
        if which == 0:
            full = nt(adv[s], xv[...])
        else:
            full = nt(auv[s], gs[...])
        lr_acc[which] += jnp.sum(jnp.where(mask(s), full.reshape(8, 16, 256), 0.0), axis=0)

    def backward(lo, hi, first):
        for g in range(lo, hi):
            for cp in ld_g[g]:
                cp.wait()
        if first:
            hg_acc[...] = jnp.zeros_like(hg_acc)

        def body(g, carry):
            hg_acc[...] += nt(gv[g], wv[g])
            return carry

        lax.fori_loop(lo, hi, body, 0)

    def psum_start(which, stage):
        lr_tx[which, stage] = lr_acc[which]
        src = lr_tx.at[which, stage]
        if stage == 0:
            return [send(src, lr_rx.at[which, 0], sib)]
        at = at_x if stage == 1 else at_y
        return [send(src, lr_rx.at[which, 3 * stage - 3 + k], at(k)) for k in (2, 1, 3)]

    def psum_end(which, stage, cps):
        for cp in cps:
            cp.wait_recv()
        if stage == 0:
            lr_acc[which] += lr_rx[which, 0]
        else:
            b = 3 * stage - 3
            lr_acc[which] += lr_rx[which, b + 1] + lr_rx[which, b + 2] + lr_rx[which, b + 3]

    h0 = ag_first(ad0, ad_hbm.at[:, pl.ds(0, 256)])
    ld_w += [load_w(g) for g in range(2, 5)]
    h1 = ag_first(ad1, ad_hbm.at[:, pl.ds(256, 256)])
    ld_x.wait()
    s0 = sib_part(0)
    ld_w += [load_w(g) for g in range(5, 8)]
    hu = ag_first(au0, au_hbm)
    matmul_half(0, 1)
    s1 = sib_part(1)
    ld_ad = load(ad_hbm, adv.at[z], lsem.at[1])
    ld_au = load(au_hbm, auv.at[z], lsem.at[2])
    ld_gs = load(g_hbm.at[:, cols(t)], gs, lsem.at[3])

    def rs_send(k):
        rs_tx[k] = (own[k] + sib_rx[k].astype(F32)).astype(BF)
        return send(rs_tx.at[k], rs_rx.at[k], at_p(OFFS[k]))

    s0.wait_recv()
    a0 = rs_send(0)
    h0 = ag_next(ad0, h0, 2)
    matmul_half(1, 1)
    s2 = sib_part(2)
    h1 = ag_next(ad1, h1, 2)
    s1.wait_recv()
    a1 = rs_send(1)
    matmul_half(2, 1)
    hu = ag_next(au0, hu, 2)
    s2.wait_recv()
    a2 = rs_send(2)
    s3 = sib_part(3)
    h0 = ag_next(ad0, h0, 3)
    lr_acc[...] = jnp.zeros_like(lr_acc)
    ld_ad.wait()
    project(0, z)
    project(0, slot(1))
    project(0, slot(7))
    h1 = ag_next(ad1, h1, 3)
    matmul_half(3, 1)
    ld_g = [load_g(g) for g in range(8)]
    hu = ag_next(au0, hu, 3)
    project(0, slot(2))
    project(0, slot(6))
    h0 = ag_next(ad0, h0, 4)
    ld_au.wait()
    ld_gs.wait()
    project(1, z)
    project(1, slot(1))
    h1 = ag_next(ad1, h1, 4)
    project(0, slot(3))
    project(0, slot(5))
    hu = ag_next(au0, hu, 4)
    project(1, slot(7))
    project(1, slot(2))
    h0 = ag_next(ad0, h0, 5)
    s3.wait_recv()
    own[3] = own[3] + sib_rx[3].astype(F32)
    h1 = ag_next(ad1, h1, 5)
    project(0, slot(4))
    lp = psum_start(0, 0)
    project(1, slot(6))
    project(1, slot(3))
    project(1, slot(5))
    hu = ag_next(au0, hu, 5)
    psum_end(0, 0, lp)
    lp = psum_start(0, 1)
    project(1, slot(4))
    bp = psum_start(1, 0)
    a0.wait_recv()
    own[3] = own[3] + rs_rx[0].astype(F32)
    psum_end(1, 0, bp)
    bp = psum_start(1, 1)
    a1.wait_recv()
    a2.wait_recv()
    p2 = []
    for k in (2, 1, 3, 0):
        at = cols(lax.rem(q + k, 4))
        both = own[3, :, at] + (rs_rx[1, :, at].astype(F32) + rs_rx[2, :, at].astype(F32))
        if k:
            p2_tx[k - 1] = both.astype(BF)
            p2.append(send(p2_tx.at[k - 1], p2_rx.at[k - 1], at_q(k)))
        else:
            r_buf[...] = both
    psum_end(0, 1, lp)
    lp = psum_start(0, 2)
    backward(0, 3, True)
    psum_end(1, 1, bp)
    bp = psum_start(1, 2)
    backward(3, 6, False)
    for cp in p2:
        cp.wait_recv()
    r_buf[...] = r_buf[...] + p2_rx[0].astype(F32) + p2_rx[1].astype(F32) + p2_rx[2].astype(F32)
    psum_end(0, 2, lp)
    def select(which):
        low = lr_acc[which].astype(BF).astype(F32)[None]
        for s in range(8):
            sel[which, pl.ds(s * 128, 128)] = (
                jnp.where(mask(s), low, 0.0).reshape(128, 256).astype(BF)
            )

    select(0)
    adapted = tn(sel[0], auv[...].reshape(1024, 256))
    mine = tid(p, q, c)
    gat[mine] = (r_buf[...] + adapted).astype(BF)

    def gather(block, device, rows=slice(None)):
        ref = gat.at[block, rows]
        return send(ref, ref, device)

    outs = []

    def put_out(block):
        outs.append(load(gat.at[block], mixed.at[:, cols(block)], osem.at[len(outs)]))

    sibs = []

    def finish(a, b):
        block = tid(p + a, q + b, c)
        sibs.append((gather(block, sib), tid(q + a, p + b, d)))
        put_out(block)

    ag_p = {0: gather(mine, at_p(1))}
    ag_m = {0: gather(mine, at_p(3))}
    ag_q = {k: gather(mine, at_q(k)) for k in (1, 3, 2)}

    def grad_part(chain, s):
        rows = pl.ds(pl.multiple_of(s * 128, 128), 128)
        if chain == 0:
            return nn(sel[0, rows], gs[...])
        return nn(sel[1, rows], xv[:, (chain - 1) * 256:chain * 256])

    def rs_start(chain):
        zr_tx[chain, 0] = grad_part(chain, slot(4)).astype(BF)
        hp = send(zr_tx.at[chain, 0, TOP], zr_rx.at[chain, 0, TOP], zp)
        hm = send(zr_tx.at[chain, 0, LOW], zr_rx.at[chain, 0, LOW], zm)
        return hp, hm

    def rs_parts(chain, ks):
        for k in ks:
            zr_own[chain, 3 - k] = grad_part(chain, slot(k))
            zr_own[chain, 6 - k] = grad_part(chain, slot(-k))

    def rs_next(chain, step, prev):
        prev[0].wait_recv()
        if step == 1:
            zr_tx[chain, 1, TOP] = (zr_own[chain, 0, TOP] + zr_rx[chain, 0, TOP].astype(F32)).astype(BF)
            zr_tx[chain, 1, LOW] = zr_own[chain, 0, LOW].astype(BF)
        else:
            zr_tx[chain, step] = (zr_own[chain, step - 1] + zr_rx[chain, step - 1].astype(F32)).astype(BF)
        hp = send(zr_tx.at[chain, step], zr_rx.at[chain, step], zp)
        prev[1].wait_recv()
        if step == 1:
            zr_tx[chain, 4, TOP] = zr_own[chain, 3, TOP].astype(BF)
            zr_tx[chain, 4, LOW] = (zr_own[chain, 3, LOW] + zr_rx[chain, 0, LOW].astype(F32)).astype(BF)
        else:
            zr_tx[chain, 3 + step] = (
                zr_own[chain, 2 + step] + zr_rx[chain, 2 + step].astype(F32)
            ).astype(BF)
        hm = send(zr_tx.at[chain, 3 + step], zr_rx.at[chain, 3 + step], zm)
        return hp, hm

    def rs_end(chain, prev):
        prev[0].wait_recv()
        prev[1].wait_recv()
        return zr_own[chain, 6] + zr_rx[chain, 3].astype(F32) + zr_rx[chain, 6].astype(F32)

    def spread(k):
        ag_p[k].wait_recv()
        bm = tid(p + 3, q + k, c)
        f1 = gather(bm, at_p(1), pl.ds(0, 128))
        finish(3, k)
        ag_m[k].wait_recv()
        bq = tid(p + 1, q + k, c)
        f2 = gather(bq, at_p(3), pl.ds(128, 128))
        finish(1, k)
        return f1, f2

    def pass_on(k):
        ag_q[k].wait_recv()
        blk = tid(p, q + 4 - k, c)
        ag_p[4 - k] = gather(blk, at_p(1))
        ag_m[4 - k] = gather(blk, at_p(3))
        finish(0, 4 - k)

    def to_sib(k):
        for cp in halves[k]:
            cp.wait_recv()
        finish(2, k)

    halves = {}
    cu = rs_start(0)
    finish(0, 0)
    psum_end(1, 2, bp)
    select(1)
    c0 = rs_start(1)
    c1 = rs_start(2)
    for chain in range(3):
        rs_parts(chain, (3,))
    backward(6, 8, False)
    cu = rs_next(0, 1, cu)
    halves[0] = spread(0)
    c0 = rs_next(1, 1, c0)
    c1 = rs_next(2, 1, c1)
    pass_on(1)
    pass_on(3)
    pass_on(2)
    for chain in range(3):
        rs_parts(chain, (2,))
    hg_bf[...] = (hg_acc[...] + tn(sel[1], adv[...].reshape(1024, 512))).astype(BF)
    st_hg = load(hg_bf, hg_out, lsem.at[5])
    cu = rs_next(0, 2, cu)
    to_sib(0)
    c0 = rs_next(1, 2, c0)
    halves[3] = spread(3)
    c1 = rs_next(2, 2, c1)
    for chain in range(3):
        rs_parts(chain, (1,))
        zr_own[chain, 6] = grad_part(chain, z)
    halves[1] = spread(1)
    halves[2] = spread(2)
    cu = rs_next(0, 3, cu)
    c0 = rs_next(1, 3, c0)
    to_sib(3)
    c1 = rs_next(2, 3, c1)
    to_sib(1)
    to_sib(2)
    ug_buf[...] = rs_end(0, cu)
    st_ug = load(ug_buf, ug_out, lsem.at[6])
    for cp, block in sibs:
        cp.wait_recv()
        put_out(block)
    dg_buf[:, 0:256] = rs_end(1, c0)
    dg_buf[:, 256:512] = rs_end(2, c1)
    st_dg = load(dg_buf, dg_out, lsem.at[7])
    for cp in sent:
        cp.wait_send()
    for cp in outs + [st_hg, st_ug, st_dg]:
        cp.wait()


def hand_over(*refs):
    sources, results, held, sems = refs[:4], refs[4:8], refs[8:12], refs[12]
    pieces = [(0, pl.ds(i * 32, 32)) for i in range(8)] + [(i, slice(None)) for i in (1, 2, 3)]
    inward = []
    for n, (i, rows) in enumerate(pieces):
        cp = pltpu.make_async_copy(sources[i].at[rows], held[i].at[rows], sems.at[0, n])
        cp.start()
        inward.append(cp)
    outward = []
    for n, (i, rows) in enumerate(pieces):
        inward[n].wait()
        cp = pltpu.make_async_copy(held[i].at[rows], results[i].at[rows], sems.at[1, n])
        cp.start()
        outward.append(cp)
    for cp in outward:
        cp.wait()


def on_device(x, g, ids, w, ad, au):
    any_spec = pl.BlockSpec(memory_space=pl.ANY)
    vmem = pl.BlockSpec(memory_space=pltpu.VMEM)
    shapes = (
        jax.ShapeDtypeStruct((256, 8192), BF),
        jax.ShapeDtypeStruct((256, 512), BF),
        jax.ShapeDtypeStruct((128, 512), F32),
        jax.ShapeDtypeStruct((128, 256), F32),
    )
    landed = pl.pallas_call(
        kernel,
        out_shape=shapes,
        in_specs=[any_spec, any_spec, vmem, any_spec, any_spec, any_spec],
        out_specs=(any_spec,) * 4,
        scratch_shapes=[
            pltpu.VMEM((256, 512), BF),
            pltpu.VMEM((256, 256), BF),
            pltpu.VMEM((8, 256, 1024), BF),
            pltpu.VMEM((8, 512, 1024), BF),
            pltpu.VMEM((8, 128, 512), BF),
            pltpu.VMEM((8, 128, 256), BF),
            pltpu.VMEM((4, 256, 1024), F32),
            pltpu.VMEM((4, 256, 1024), BF),
            pltpu.VMEM((4, 256, 1024), BF),
            pltpu.VMEM((3, 256, 1024), BF),
            pltpu.VMEM((3, 256, 1024), BF),
            pltpu.VMEM((256, 256), F32),
            pltpu.VMEM((3, 256, 256), BF),
            pltpu.VMEM((3, 256, 256), BF),
            pltpu.VMEM((32, 256, 256), BF),
            pltpu.VMEM((256, 512), F32),
            pltpu.VMEM((256, 512), BF),
            pltpu.VMEM((2, 16, 256), F32),
            pltpu.VMEM((2, 3, 16, 256), F32),
            pltpu.VMEM((2, 7, 16, 256), F32),
            pltpu.VMEM((2, 1024, 256), BF),
            pltpu.VMEM((3, 7, 128, 256), F32),
            pltpu.VMEM((3, 7, 128, 256), BF),
            pltpu.VMEM((3, 7, 128, 256), BF),
            pltpu.VMEM((128, 512), F32),
            pltpu.VMEM((128, 256), F32),
            pltpu.SemaphoreType.DMA((8,)),
            pltpu.SemaphoreType.DMA((32,)),
            pltpu.SemaphoreType.DMA((32,)),
            pltpu.SemaphoreType.DMA((32,)),
            pltpu.SemaphoreType.DMA((NSEM,)),
            pltpu.SemaphoreType.DMA((NSEM,)),
        ],
        compiler_params=pltpu.CompilerParams(
            collective_id=0, has_side_effects=True, vmem_limit_bytes=56 * 2**20
        ),
    )(x, g, ids.reshape(1, 256), w, ad.reshape(128, 512), au.reshape(128, 256))
    mixed, hg, dg, ug = pl.pallas_call(
        hand_over,
        out_shape=shapes,
        in_specs=[any_spec] * 4,
        out_specs=(any_spec,) * 4,
        scratch_shapes=[pltpu.VMEM(one.shape, one.dtype) for one in shapes]
        + [pltpu.SemaphoreType.DMA((2, 11))],
        compiler_params=pltpu.CompilerParams(vmem_limit_bytes=60 * 2**20),
    )(*landed)
    return mixed, hg, dg.reshape(8, 16, 512), ug.reshape(8, 16, 256)


def solution(mesh):
    return jax.shard_map(
        on_device,
        mesh=mesh,
        in_specs=(
            P("adapter", "tensor"),
            P("adapter", None),
            P("adapter"),
            P("tensor", None),
            P("adapter", None, "tensor"),
            P("adapter", None, "tensor"),
        ),
        out_specs=(
            P("adapter", None),
            P("adapter", "tensor"),
            P("adapter", None, "tensor"),
            P("adapter", None, "tensor"),
        ),
        check_vma=False,
    )
```
